32 devices in a mesh: dp: 4 (over y, core), seq: 8 (over z, x).
Axes of the slice: x: 2, y: 2, z: 4, core: 2. Of those that a mesh axis runs over, the one named last changes fastest.
Arguments:
- glu_out: bfloat16 [4, 1024, 1536], P('dp', 'seq'), may hold values from -8 to 8
- conv_weight: float32 [32, 1536], replicated, may hold values from -1 to 1
- bn_gain: float32 [16, 1536], replicated, may hold values from 0.25 to 1.75
- bn_bias: float32 [16, 1536], replicated, may hold values from -3 to 3
- w_out: bfloat16 [1536, 1536], P(('dp', 'seq')), may hold values from -0.15625 to 0.15625
- cotangent: bfloat16 [4, 1024, 1536], P('dp', 'seq'), may hold values from -8 to 8
- language: int32 [4], P('dp'), may hold values from 0 to 15
- length: int32 [4], P('dp'), may hold values from 256 to 1024, as said below
Outputs:
- block_out: bfloat16 [4, 1024, 1536], P('dp', 'seq')
- weight_grad: float32 [1536, 1536], P(('dp', 'seq'))
- input_grad: bfloat16 [4, 1024, 1536], P('dp', 'seq')
The draws below stay inside these ranges and needn't reach their ends.
Inputs may be any that keep to these rules, and one draw needn't show every extreme that they name: Each length is a multiple of 256; at least one utterance is valid over all 1024 frames.
All inputs are finite; a program needn't handle non-finite values.
Results may differ from the reference program's by a relative error of at most 0.0095.
Values may be sent and summed in bfloat16 or wider, within the bound.
A program may use at most 64 MiB of HBM per device.

```python
import jax
import jax.numpy as jnp
from jax import lax

D = 1536
KERNEL = 32
LANGS = 16
STEP = 256
UTT_DEV = 1
FRM_DEV = 128
UTTS = 4
FRAMES = 1024


def draw_length(key, part):
    blocks = FRAMES // STEP
    picked = jax.random.randint(jax.random.fold_in(key, 11), (UTTS,), 1, blocks + 1)
    longest = jax.random.randint(jax.random.fold_in(key, 12), (), 0, UTTS)
    picked = jnp.where(jnp.arange(UTTS, dtype=jnp.int32) == longest, blocks, picked)
    return (picked * STEP).astype(jnp.int32)


def steady_part(key, offset_scale, drift_scale):
    offset = jax.random.normal(jax.random.fold_in(key, 21), (UTTS, 1, D), jnp.float32)
    drift = jax.random.normal(jax.random.fold_in(key, 22), (UTTS, 1, D), jnp.float32)
    ramp = (jnp.arange(FRAMES, dtype=jnp.float32) * (2.0 / FRAMES) - 1.0)[None, :, None]
    return offset_scale * offset + drift_scale * drift * ramp


def rough_part(key):
    noise = jax.random.normal(jax.random.fold_in(key, 31), (UTTS, FRAMES, D), jnp.float32)
    return jnp.clip(noise, -6.0, 6.0)


def draw_glu_out(key, part):
    common = steady_part(jax.random.fold_in(key, 41), 0.5, 0.5)
    total = rough_part(jax.random.fold_in(key, 42)) + common
    return jnp.clip(total, -8.0, 8.0).astype(jnp.bfloat16)


def draw_cotangent(key, part):
    common = steady_part(jax.random.fold_in(key, 51), 0.5, 0.5)
    rough = rough_part(jax.random.fold_in(key, 52))
    groups = UTTS * FRAMES // (UTT_DEV * FRM_DEV)
    width = D // groups
    order = jax.random.permutation(jax.random.fold_in(key, 53), groups)
    utt_index = jnp.arange(UTTS, dtype=jnp.int32)[:, None, None]
    frame_index = jnp.arange(FRAMES, dtype=jnp.int32)[None, :, None]
    group = utt_index // UTT_DEV * (FRAMES // FRM_DEV) + frame_index // FRM_DEV
    column_block = (jnp.arange(D, dtype=jnp.int32) // width)[None, None, :]
    factor = jnp.where(order[group] == column_block, 4.0, 1.0)
    total = rough * factor + common
    return jnp.clip(total, -8.0, 8.0).astype(jnp.bfloat16)


def set_ends(entries, own_key, smallest, high):
    dims = entries.shape
    index_at = [jax.random.randint(jax.random.fold_in(own_key, axis), (), 0, dims[axis]) for axis in range(len(dims))]
    entries = entries.at[tuple(index_at)].set(smallest)
    longest = dims.index(max(dims))
    index_at[longest] = (index_at[longest] + 1) % dims[longest]
    return entries.at[tuple(index_at)].set(high)


def block_scale(own_key, shape, shards, smallest, largest):
    gain = 1.0
    for dim, blocks in shards:
        draws = jax.random.uniform(jax.random.fold_in(jax.random.fold_in(own_key, 6), dim), (blocks,), jnp.float32, smallest / len(shards), largest / len(shards))
        gain = gain * jnp.repeat(jnp.exp(draws), shape[dim] // blocks).reshape((-1,) + (1,) * (len(shape) - 1 - dim))
    return gain


def gaussian(key, extent, scale, most, split=(), kind=jnp.bfloat16):
    gain = block_scale(key, extent, split, -0.22, 0.18) if split else 1.0
    result = jax.random.normal(key, extent, jnp.float32) * scale * gain
    return jnp.minimum(jnp.maximum(result, -most), most).astype(kind)


def setup_inputs(seed: int = 0) -> dict:
    key_of = jax.random.split(jax.random.key(seed), 9)
    return {
        "glu_out": draw_glu_out(jax.random.fold_in(key_of[8], 71), 0),
        "conv_weight": gaussian(key_of[1], (KERNEL, D), KERNEL ** -0.5, 1.0, (), jnp.float32),
        "bn_gain": jnp.clip(1.0 + 0.15 * jax.random.normal(key_of[2], (LANGS, D), jnp.float32), 0.25, 1.75),
        "bn_bias": gaussian(key_of[3], (LANGS, D), 0.5, 3.0, (), jnp.float32),
        "w_out": gaussian(key_of[4], (D, D), D ** -0.5, 0.15625, ((0, 32),)),
        "cotangent": draw_cotangent(jax.random.fold_in(key_of[8], 71), 0),
        "language": set_ends(jax.random.randint(key_of[6], (UTTS,), 0, LANGS), jax.random.fold_in(key_of[6], 1), 0, LANGS - 1).astype(jnp.int32),
        "length": draw_length(jax.random.fold_in(key_of[8], 71), 0),
    }


epsilon = 1e-05

def depthwise(padded, taps, frames):
    running = jnp.zeros((frames, padded.shape[1]), jnp.float32)
    for offset in range(taps.shape[0]):
        running = running + padded[offset:offset + frames].astype(jnp.float32) * taps[offset]
    return running

def prepare(glu_row, length_row, conv_weight):
    valid = (jnp.arange(FRAMES, dtype=jnp.int32) < length_row).astype(jnp.float32)[:, None]
    masked = glu_row * valid.astype(jnp.bfloat16)
    half_width = KERNEL // 2
    padded = jnp.pad(masked, ((half_width, half_width - 1), (0, 0)))
    return (depthwise(padded, conv_weight, FRAMES), valid)

def reference(glu_out, conv_weight, bn_gain, bn_bias, w_out, cotangent, language, length):
    half_width = KERNEL // 2
    one_hot = (language[:, None] == jnp.arange(LANGS, dtype=jnp.int32)[None, :]).astype(jnp.float32)

    def first_pass(inputs):
        convolved, valid = prepare(inputs[0], inputs[1], conv_weight)
        return lax.optimization_barrier(jnp.sum(convolved * valid, axis=0))
    sums = lax.map(first_pass, (glu_out, length))
    counts = jnp.dot(one_hot.T, length.astype(jnp.float32), precision=lax.Precision.HIGHEST)
    denominator = jnp.maximum(counts, 1.0)[:, None]
    average = jnp.dot(one_hot.T, sums, precision=lax.Precision.HIGHEST) / denominator
    average_rows = average[language]

    def second_pass(inputs):
        convolved, valid = prepare(inputs[0], inputs[1], conv_weight)
        centred = (convolved - inputs[2]) * valid
        return lax.optimization_barrier(jnp.sum(centred * centred, axis=0))
    spread = lax.map(second_pass, (glu_out, length, average_rows))
    variance = jnp.dot(one_hot.T, spread, precision=lax.Precision.HIGHEST) / denominator
    inverse_std = lax.rsqrt(variance + epsilon)
    inverse_rows = inverse_std[language]
    gain_rows = bn_gain[language]
    bias_rows = bn_bias[language]

    def third_pass(carry, inputs):
        glu_row, length_row, grad_row, average_row, inverse_row, gain_row, bias_row = inputs
        convolved, valid = prepare(glu_row, length_row, conv_weight)
        normed = (convolved - average_row) * inverse_row
        pre_act = normed * gain_row + bias_row
        sigmoid_act = jax.nn.sigmoid(pre_act)
        active = (pre_act * sigmoid_act * valid).astype(jnp.bfloat16)
        output = jnp.dot(active, w_out, preferred_element_type=jnp.float32).astype(jnp.bfloat16)
        back_proj = lax.dot_general(grad_row, w_out, (((1,), (1,)), ((), ())), preferred_element_type=jnp.float32)
        grad_pre = back_proj * valid * sigmoid_act * (1.0 + pre_act * (1.0 - sigmoid_act))
        grad_normed = grad_pre * gain_row
        carry = carry + lax.dot_general(active, grad_row, (((0,), (0,)), ((), ())), preferred_element_type=jnp.float32)
        return (carry, (output, grad_normed, lax.optimization_barrier(jnp.sum(grad_normed, axis=0)), lax.optimization_barrier(jnp.sum(grad_normed * normed, axis=0))))
    weight_grad, (block_out, grad_all, first_rows, second_rows) = lax.scan(third_pass, jnp.zeros((D, D), jnp.float32), (glu_out, length, cotangent, average_rows, inverse_rows, gain_rows, bias_rows))
    first_sum = jnp.dot(one_hot.T, first_rows, precision=lax.Precision.HIGHEST) / denominator
    second_sum = jnp.dot(one_hot.T, second_rows, precision=lax.Precision.HIGHEST) / denominator

    def fourth_pass(inputs):
        glu_row, length_row, grad_normed, average_row, inverse_row, first_row, second_row = inputs
        convolved, valid = prepare(glu_row, length_row, conv_weight)
        normed = (convolved - average_row) * inverse_row
        grad_conv = (valid * inverse_row * (grad_normed - first_row - normed * second_row)).astype(jnp.bfloat16)
        padded = jnp.pad(grad_conv, ((half_width - 1, half_width), (0, 0)))
        return (depthwise(padded, conv_weight[::-1], FRAMES) * valid).astype(jnp.bfloat16)
    input_grad = lax.map(fourth_pass, (glu_out, length, grad_all, average_rows, inverse_rows, first_sum[language], second_sum[language]))
    return (block_out, weight_grad, input_grad)
```

```python
import jax
import jax.numpy as jnp
from jax import lax
from jax.experimental import pallas as pl
from jax.experimental.pallas import tpu as pltpu
from jax.sharding import PartitionSpec as P

LANGS = 16


epsilon = 1e-05


def with_halo(array, sides, width):
    for axis, dim in sides:
        size, length = (lax.axis_size(axis), array.shape[dim])
        up = [(i, (i + 1) % size) for i in range(size - 1)]
        down = [(j, i) for i, j in up]
        last = lax.slice_in_dim(array, length - width, length, axis=dim)
        first = lax.slice_in_dim(array, 0, width, axis=dim)
        before = lax.ppermute(last, axis, up)
        after = lax.ppermute(first, axis, down)
        array = jnp.concatenate([before, array, after], axis=dim)
    return array


def depthwise(padded, taps, frames):
    running = jnp.zeros((padded.shape[0], frames, padded.shape[2]), jnp.float32)
    for offset in range(taps.shape[0]):
        running = running + padded[:, offset : offset + frames].astype(jnp.float32) * taps[offset]
    return running


def with_rim(values, half_width):
    return with_halo(values, (("seq", 1),), half_width)


def per_language(one_hot, values_table):
    return jnp.dot(one_hot.T, values_table, precision=lax.Precision.HIGHEST)


def per_utterance(one_hot, values_table):
    return jnp.dot(one_hot, values_table, precision=lax.Precision.HIGHEST)[:, None, :]


def on_device(glu_out, conv_weight, bn_gain, bn_bias, w_out, cotangent, language, length):
    utterances, frames, channels = glu_out.shape
    kernel = conv_weight.shape[0]
    half_width = kernel // 2
    position = lax.axis_index("seq") * frames + lax.iota(jnp.int32, frames)
    valid = (position[None, :] < length[:, None]).astype(jnp.float32)[:, :, None]
    one_hot = (language[:, None] == lax.iota(jnp.int32, LANGS)[None, :]).astype(jnp.float32)
    masked = glu_out * valid.astype(jnp.bfloat16)
    extended = with_rim(masked, half_width)
    convolved = depthwise(extended[:, : frames + kernel - 1], conv_weight, frames)
    counts = per_language(one_hot, jnp.sum(valid, axis=(1, 2)))
    local_sum = per_language(one_hot, jnp.sum(convolved * valid, axis=1))
    local_square = per_language(one_hot, jnp.sum(convolved * convolved * valid, axis=1))
    total_sum, total_square, total_count = lax.psum(
        (local_sum, local_square, counts), ("dp", "seq")
    )
    denominator = jnp.maximum(total_count, 1.0)[:, None]
    average = total_sum / denominator
    variance = total_square / denominator - average * average
    average_utt = per_utterance(one_hot, average)
    inverse_utt = per_utterance(one_hot, lax.rsqrt(variance + epsilon))
    gain_utt = per_utterance(one_hot, bn_gain)
    bias_utt = per_utterance(one_hot, bn_bias)
    normed = (convolved - average_utt) * inverse_utt
    pre_act = normed * gain_utt + bias_utt
    sigmoid_act = jax.nn.sigmoid(pre_act)
    active = (pre_act * sigmoid_act * valid).astype(jnp.bfloat16)
    full_weight = lax.all_gather(w_out, ("dp", "seq"), axis=0, tiled=True)
    flat_active = active.reshape(utterances * frames, channels)
    flat_grad = cotangent.reshape(utterances * frames, channels)
    output = jnp.dot(flat_active, full_weight, preferred_element_type=jnp.float32)
    output = output.astype(jnp.bfloat16).reshape(utterances, frames, channels)
    back_proj = lax.dot_general(
        flat_grad, full_weight, (((1,), (1,)), ((), ())), preferred_element_type=jnp.float32
    )
    back_proj = back_proj.reshape(utterances, frames, channels)
    grad_pre = back_proj * valid * sigmoid_act * (1.0 + pre_act * (1.0 - sigmoid_act))
    grad_normed = grad_pre * gain_utt
    first_sum, second_sum = lax.psum(
        (
            per_language(one_hot, jnp.sum(grad_normed, axis=1)),
            per_language(one_hot, jnp.sum(grad_normed * normed, axis=1)),
        ),
        ("dp", "seq"),
    )
    shift_term = per_utterance(one_hot, first_sum / denominator)
    scale_term = per_utterance(one_hot, second_sum / denominator)
    grad_conv = (valid * inverse_utt * (grad_normed - shift_term - normed * scale_term)).astype(
        jnp.bfloat16
    )
    rim_grad = with_rim(grad_conv, half_width)
    input_grad = (depthwise(rim_grad[:, 1:], conv_weight[::-1], frames) * valid).astype(
        jnp.bfloat16
    )
    weight_grad = lax.psum_scatter(
        lax.dot_general(
            flat_active, flat_grad, (((0,), (0,)), ((), ())), preferred_element_type=jnp.float32
        ),
        ("dp", "seq"),
        scatter_dimension=0,
        tiled=True,
    )
    return (output, weight_grad, input_grad)


MESH = pl.DeviceIdType.MESH
LANE = 128


def tile(c):
    return pl.ds(pl.multiple_of(c * LANE, LANE), LANE)


def fused(
    lang_ref, len_ref, x_ref, tap_ref, gain_ref, bias_ref, w_ref, cot_ref,
    out_ref, wg_ref, ig_ref,
    wfull, cotg, act, act_t, ag, part, ysum, yin, zin,
    ext, xf, normed, slope, gext,
    info, info_in, stat, stat_in, stat_mid, stat_dp, stat_res,
    send, recv,
):
    frames, channels = x_ref.shape
    taps = tap_ref.shape[0]
    half = taps // 2
    chunks = channels // LANE
    dp, seq = lax.axis_index("dp"), lax.axis_index("seq")
    y, c, z, x = dp // 2, dp % 2, seq // 2, seq % 2
    seq_x, dp_c, dp_y = seq + 1 - 2 * x, dp + 1 - 2 * c, dp + 2 - 4 * y
    to_x, to_c, to_y, to_cx = (dp, seq_x), (dp_c, seq), (dp_y, seq), (dp_c, seq_x)
    xn, cn, yn = 1 - x, 1 - c, 1 - y
    seq_peers = [(dp, (seq + d) % 8) for d in range(1, 8)]
    dp_peers = [((dp + d) % 4, seq) for d in range(1, 4)]
    z_peers = [(z + d) % 4 for d in range(1, 4)]
    lang, length = lang_ref[0], len_ref[0]

    barrier = pltpu.get_barrier_semaphore()
    greet = seq_peers + dp_peers + [to_cx]
    for peer in greet:
        pl.semaphore_signal(barrier, inc=1, device_id=peer, device_id_type=MESH)

    info[0:8, :] = jnp.full((8, LANE), lang, jnp.int32)
    info[8:16, :] = jnp.full((8, LANE), length, jnp.int32)
    wfull[dp, z, x] = w_ref[...]
    cotg[0] = cot_ref[...]
    pl.semaphore_wait(barrier, len(greet))

    pending = []
    count = [0]

    def push(src, dst, peer):
        i = count[0]
        count[0] += 1
        copy = pltpu.make_async_remote_copy(
            src_ref=src, dst_ref=dst, send_sem=send.at[i], recv_sem=recv.at[i],
            device_id=peer, device_id_type=MESH,
        )
        copy.start()
        pending.append(copy)
        return copy

    seq_up, seq_down = (dp, (seq + 1) % 8), (dp, (seq + 7) % 8)
    halo = [
        push(x_ref.at[frames - half : frames], ext.at[0:half], seq_up),
        push(x_ref.at[0:half], ext.at[half + frames : frames + 2 * half], seq_down),
    ]
    w_z = [push(w_ref, wfull.at[dp, z, x], (dp, zp * 2 + x)) for zp in z_peers]
    cot_x = push(cot_ref, cotg.at[1], to_x)
    cot_c = push(cot_ref, cotg.at[2], to_c)
    told = [push(info, info_in.at[d], peer) for d, peer in enumerate(dp_peers)]

    row = lax.broadcasted_iota(jnp.int32, (frames + 2 * half, LANE), 0) + (seq * frames - half)
    inside = (row >= 0) & (row < length)
    valid = inside[half : half + frames].astype(jnp.float32)

    ext[half : half + frames, :] = x_ref[...]
    for copy in halo:
        copy.wait_recv()

    def conv_step(i, carry):
        t = tile(i)
        xf[:, t] = jnp.where(inside, ext[:, t].astype(jnp.float32), 0.0)
        weights = tap_ref[:, t]
        total = jnp.zeros((frames, LANE), jnp.float32)
        for k in range(taps):
            total = total + xf[k : k + frames, t] * weights[k : k + 1]
        normed[:, t] = total
        kept = total * valid
        stat[0, pl.ds(i, 1), :] = jnp.sum(kept, axis=0, keepdims=True)
        stat[0, pl.ds(chunks + i, 1), :] = jnp.sum(kept * total, axis=0, keepdims=True)
        return carry

    lax.fori_loop(0, chunks, conv_step, 0)

    def sum_seq(n):
        return [push(stat.at[n], stat_in.at[n, d], peer) for d, peer in enumerate(seq_peers)]

    def sum_dp(n, copies):
        for copy in copies:
            copy.wait_recv()
        total = stat[n]
        for d in range(7):
            total = total + stat_in[n, d]
        stat_mid[n] = total
        return [push(stat_mid.at[n], stat_dp.at[n, d], peer) for d, peer in enumerate(dp_peers)]

    def finish(n, copies):
        for copy in copies:
            copy.wait_recv()
        total = stat_mid[n]
        frames_of = jnp.full((1, LANE), length, jnp.int32).astype(jnp.float32)
        for d in range(3):
            same = (info_in[d, 0:1, :] == lang).astype(jnp.float32)
            total = total + stat_dp[n, d] * same
            frames_of = frames_of + info_in[d, 8:9, :].astype(jnp.float32) * same
        return total / jnp.maximum(frames_of, 1.0)

    first = sum_seq(0)

    for copy in w_z:
        copy.wait_recv()
    w_x = push(wfull.at[dp, :, x], wfull.at[dp, :, x], to_x)
    w_y = push(wfull.at[dp, :, x], wfull.at[dp, :, x], to_y)
    w_core = [push(wfull.at[dp, :, x], wfull.at[dp, :, x], to_c)]

    first = sum_dp(0, first)
    cot_x.wait_recv()
    cot_cx = push(cotg.at[1], cotg.at[3], to_c)
    for copy in told:
        copy.wait_recv()
    mean = finish(0, first)
    average = mean[0:chunks]
    variance = mean[chunks : 2 * chunks] - average * average
    stat_res[0, 0:chunks, :] = average
    stat_res[0, chunks : 2 * chunks, :] = lax.rsqrt(variance + epsilon)

    mine = lax.broadcasted_iota(jnp.int32, (LANGS, LANE), 0) == lang

    def act_step(i, carry):
        t = tile(i)
        average = stat_res[0, pl.ds(i, 1), :]
        inverse = stat_res[0, pl.ds(chunks + i, 1), :]
        gain = jnp.sum(jnp.where(mine, gain_ref[:, t], 0.0), axis=0, keepdims=True)
        bias = jnp.sum(jnp.where(mine, bias_ref[:, t], 0.0), axis=0, keepdims=True)
        norm = (normed[:, t] - average) * inverse
        pre = norm * gain + bias
        s = jax.nn.sigmoid(pre)
        normed[:, t] = norm
        slope[:, t] = valid * s * (1.0 + pre * (1.0 - s)) * gain
        act[:, t] = (pre * s * valid).astype(jnp.bfloat16)
        return carry

    lax.fori_loop(0, chunks, act_step, 0)

    group = channels // 4
    rows = wg_ref.shape[0]
    for g in range(4):
        turned = jnp.transpose(act[:, g * group : (g + 1) * group].astype(jnp.float32))
        act_t[g // 2, g % 2] = turned.astype(jnp.bfloat16).reshape(4, 2, rows, frames)

    factors = [
        push(act_t.at[:, cc, :, xx], ag.at[slot], peer)
        for slot, cc, xx, peer in ((1, c, xn, to_x), (2, cn, x, to_c), (3, cn, xn, to_cx))
    ]
    ag[0] = act_t[:, c, :, x]

    mid = channels // 2
    w_x.wait_recv()
    w_yd = push(wfull.at[dp, :, xn, :, mid:], wfull.at[dp, :, xn, :, mid:], to_y)
    w_core.append(push(wfull.at[dp, :, xn], wfull.at[dp, :, xn], to_c))
    w_y.wait_recv()
    w_xd = push(wfull.at[dp_y, :, x, :, :mid], wfull.at[dp_y, :, x, :, :mid], to_x)
    w_core.append(push(wfull.at[dp_y, :, x], wfull.at[dp_y, :, x], to_c))

    cot_c.wait_recv()
    cot_cx.wait_recv()
    for copy in factors:
        copy.wait_recv()
    lhs = jnp.concatenate([ag[s].reshape(8 * rows, frames) for s in range(4)], axis=1)
    rhs = cotg.reshape(4 * frames, channels)

    def grad_step(i, carry):
        t = pl.ds(pl.multiple_of(i * 256, 256), 256)
        value = jnp.dot(lhs, rhs[:, t], preferred_element_type=jnp.float32)
        part[:, :, :, t] = value.astype(jnp.bfloat16).reshape(2, 4, rows, 256)
        return carry

    lax.fori_loop(0, channels // 256, grad_step, 0)
    order = z_peers + [z]
    over_y = [
        push(part.at[yn, zp], yin.at[d], to_y) for d, zp in enumerate(order)
    ]

    w_xd.wait_recv()
    w_yd.wait_recv()
    w_core.append(push(wfull.at[dp_y, :, xn], wfull.at[dp_y, :, xn], to_c))

    over_z = []
    for d, zp in enumerate(order):
        over_y[d].wait_recv()
        added = part[y, zp].astype(jnp.float32) + yin[d].astype(jnp.float32)
        if d < 3:
            ysum[d] = added.astype(jnp.bfloat16)
            over_z.append(push(ysum.at[d], zin.at[d], (dp, zp * 2 + x)))
        else:
            wg_ref[...] = added

    for copy in w_core:
        copy.wait_recv()
    weight = wfull.reshape(channels, channels)

    def back_step(i, carry):
        t = pl.ds(pl.multiple_of(i * 256, 256), 256)
        back = lax.dot_general(
            cot_ref[...], weight[t, :], (((1,), (1,)), ((), ())),
            preferred_element_type=jnp.float32,
        )
        grad = back * slope[:, t]
        slope[:, t] = grad
        one = jnp.sum(grad, axis=0, keepdims=True)
        two = jnp.sum(grad * normed[:, t], axis=0, keepdims=True)
        for j in range(2):
            cut = slice(j * LANE, (j + 1) * LANE)
            stat[1, pl.ds(2 * i + j, 1), :] = one[:, cut]
            stat[1, pl.ds(chunks + 2 * i + j, 1), :] = two[:, cut]
        return carry

    lax.fori_loop(0, channels // 256, back_step, 0)
    second = sum_seq(1)

    def out_step(i, carry):
        t = pl.ds(pl.multiple_of(i * 256, 256), 256)
        value = jnp.dot(act[...], weight[:, t], preferred_element_type=jnp.float32)
        out_ref[:, t] = value.astype(jnp.bfloat16)
        return carry

    lax.fori_loop(0, channels // 256, out_step, 0)
    second = sum_dp(1, second)
    stat_res[1] = finish(1, second)

    def grad_conv_step(i, carry):
        t = tile(i)
        inverse = stat_res[0, pl.ds(chunks + i, 1), :]
        shift = stat_res[1, pl.ds(i, 1), :]
        scale = stat_res[1, pl.ds(chunks + i, 1), :]
        grad = valid * inverse * (slope[:, t] - shift - normed[:, t] * scale)
        gext[half : half + frames, t] = grad.astype(jnp.bfloat16)
        return carry

    lax.fori_loop(0, chunks, grad_conv_step, 0)
    halo = [
        push(gext.at[frames : frames + half], gext.at[0:half], seq_up),
        push(gext.at[half : 2 * half], gext.at[half + frames : frames + 2 * half], seq_down),
    ]
    total = wg_ref[...]
    for d, copy in enumerate(over_z):
        copy.wait_recv()
        total = total + zin[d].astype(jnp.float32)
    wg_ref[...] = total
    for copy in halo:
        copy.wait_recv()

    def input_step(i, carry):
        t = tile(i)
        xf[:, t] = jnp.where(inside, gext[:, t].astype(jnp.float32), 0.0)
        weights = tap_ref[:, t]
        total = jnp.zeros((frames, LANE), jnp.float32)
        for k in range(taps):
            total = total + xf[2 * half - k : 2 * half - k + frames, t] * weights[k : k + 1]
        ig_ref[:, t] = (total * valid).astype(jnp.bfloat16)
        return carry

    lax.fori_loop(0, chunks, input_step, 0)
    for copy in pending:
        copy.wait_send()


COPIES = 64


def on_device_fused(glu_out, conv_weight, bn_gain, bn_bias, w_out, cotangent, language, length):
    _, frames, channels = glu_out.shape
    rows = w_out.shape[0]
    half = conv_weight.shape[0] // 2
    bf16, f32 = jnp.bfloat16, jnp.float32
    stats = 2 * channels // LANE
    vmem = pl.BlockSpec(memory_space=pltpu.VMEM)
    smem = pl.BlockSpec(memory_space=pltpu.SMEM)
    block_out, weight_grad, input_grad = pl.pallas_call(
        fused,
        out_shape=(
            jax.ShapeDtypeStruct((frames, channels), bf16),
            jax.ShapeDtypeStruct((rows, channels), f32),
            jax.ShapeDtypeStruct((frames, channels), bf16),
        ),
        in_specs=[smem, smem] + [vmem] * 6,
        out_specs=(vmem, vmem, vmem),
        scratch_shapes=[
            pltpu.VMEM((4, 4, 2, rows, channels), bf16),
            pltpu.VMEM((4, frames, channels), bf16),
            pltpu.VMEM((frames, channels), bf16),
            pltpu.VMEM((2, 2, 4, 2, rows, frames), bf16),
            pltpu.VMEM((4, 2, 4, rows, frames), bf16),
            pltpu.VMEM((2, 4, rows, channels), bf16),
            pltpu.VMEM((3, rows, channels), bf16),
            pltpu.VMEM((4, rows, channels), bf16),
            pltpu.VMEM((3, rows, channels), bf16),
            pltpu.VMEM((frames + 2 * half, channels), bf16),
            pltpu.VMEM((frames + 2 * half, channels), f32),
            pltpu.VMEM((frames, channels), f32),
            pltpu.VMEM((frames, channels), f32),
            pltpu.VMEM((frames + 2 * half, channels), bf16),
            pltpu.VMEM((16, LANE), jnp.int32),
            pltpu.VMEM((3, 16, LANE), jnp.int32),
            pltpu.VMEM((2, stats, LANE), f32),
            pltpu.VMEM((2, 7, stats, LANE), f32),
            pltpu.VMEM((2, stats, LANE), f32),
            pltpu.VMEM((2, 3, stats, LANE), f32),
            pltpu.VMEM((2, stats, LANE), f32),
            pltpu.SemaphoreType.DMA((COPIES,)),
            pltpu.SemaphoreType.DMA((COPIES,)),
        ],
        compiler_params=pltpu.CompilerParams(
            collective_id=0, has_side_effects=True, vmem_limit_bytes=48 * 1024 * 1024
        ),
    )(language, length, glu_out[0], conv_weight, bn_gain, bn_bias, w_out, cotangent[0])
    return block_out[None], weight_grad, input_grad[None]


def solution(mesh):
    placed = (
        P("dp", "seq", None),
        P(),
        P(),
        P(),
        P(("dp", "seq"), None),
        P("dp", "seq", None),
        P("dp"),
        P("dp"),
    )
    small = mesh.shape["dp"] == 4 and mesh.shape["seq"] == 8
    return jax.shard_map(
        on_device_fused if small else on_device,
        mesh=mesh,
        in_specs=placed,
        out_specs=(P("dp", "seq", None), P(("dp", "seq"), None), P("dp", "seq", None)),
        check_vma=False,
    )
```

```python
import jax
import jax.numpy as jnp
from jax import lax
from jax.experimental import pallas as pl
from jax.experimental.pallas import tpu as pltpu
from jax.sharding import PartitionSpec as P

LANGS = 16


epsilon = 1e-05


def with_halo(array, sides, width):
    for axis, dim in sides:
        size, length = (lax.axis_size(axis), array.shape[dim])
        up = [(i, (i + 1) % size) for i in range(size - 1)]
        down = [(j, i) for i, j in up]
        last = lax.slice_in_dim(array, length - width, length, axis=dim)
        first = lax.slice_in_dim(array, 0, width, axis=dim)
        before = lax.ppermute(last, axis, up)
        after = lax.ppermute(first, axis, down)
        array = jnp.concatenate([before, array, after], axis=dim)
    return array


def depthwise(padded, taps, frames):
    running = jnp.zeros((padded.shape[0], frames, padded.shape[2]), jnp.float32)
    for offset in range(taps.shape[0]):
        running = running + padded[:, offset : offset + frames].astype(jnp.float32) * taps[offset]
    return running


def with_rim(values, half_width):
    return with_halo(values, (("seq", 1),), half_width)


def per_language(one_hot, values_table):
    return jnp.dot(one_hot.T, values_table, precision=lax.Precision.HIGHEST)


def per_utterance(one_hot, values_table):
    return jnp.dot(one_hot, values_table, precision=lax.Precision.HIGHEST)[:, None, :]


def on_device(glu_out, conv_weight, bn_gain, bn_bias, w_out, cotangent, language, length):
    utterances, frames, channels = glu_out.shape
    kernel = conv_weight.shape[0]
    half_width = kernel // 2
    position = lax.axis_index("seq") * frames + lax.iota(jnp.int32, frames)
    valid = (position[None, :] < length[:, None]).astype(jnp.float32)[:, :, None]
    one_hot = (language[:, None] == lax.iota(jnp.int32, LANGS)[None, :]).astype(jnp.float32)
    masked = glu_out * valid.astype(jnp.bfloat16)
    extended = with_rim(masked, half_width)
    convolved = depthwise(extended[:, : frames + kernel - 1], conv_weight, frames)
    counts = per_language(one_hot, jnp.sum(valid, axis=(1, 2)))
    local_sum = per_language(one_hot, jnp.sum(convolved * valid, axis=1))
    local_square = per_language(one_hot, jnp.sum(convolved * convolved * valid, axis=1))
    total_sum, total_square, total_count = lax.psum(
        (local_sum, local_square, counts), ("dp", "seq")
    )
    denominator = jnp.maximum(total_count, 1.0)[:, None]
    average = total_sum / denominator
    variance = total_square / denominator - average * average
    average_utt = per_utterance(one_hot, average)
    inverse_utt = per_utterance(one_hot, lax.rsqrt(variance + epsilon))
    gain_utt = per_utterance(one_hot, bn_gain)
    bias_utt = per_utterance(one_hot, bn_bias)
    normed = (convolved - average_utt) * inverse_utt
    pre_act = normed * gain_utt + bias_utt
    sigmoid_act = jax.nn.sigmoid(pre_act)
    active = (pre_act * sigmoid_act * valid).astype(jnp.bfloat16)
    full_weight = lax.all_gather(w_out, ("dp", "seq"), axis=0, tiled=True)
    flat_active = active.reshape(utterances * frames, channels)
    flat_grad = cotangent.reshape(utterances * frames, channels)
    output = jnp.dot(flat_active, full_weight, preferred_element_type=jnp.float32)
    output = output.astype(jnp.bfloat16).reshape(utterances, frames, channels)
    back_proj = lax.dot_general(
        flat_grad, full_weight, (((1,), (1,)), ((), ())), preferred_element_type=jnp.float32
    )
    back_proj = back_proj.reshape(utterances, frames, channels)
    grad_pre = back_proj * valid * sigmoid_act * (1.0 + pre_act * (1.0 - sigmoid_act))
    grad_normed = grad_pre * gain_utt
    first_sum, second_sum = lax.psum(
        (
            per_language(one_hot, jnp.sum(grad_normed, axis=1)),
            per_language(one_hot, jnp.sum(grad_normed * normed, axis=1)),
        ),
        ("dp", "seq"),
    )
    shift_term = per_utterance(one_hot, first_sum / denominator)
    scale_term = per_utterance(one_hot, second_sum / denominator)
    grad_conv = (valid * inverse_utt * (grad_normed - shift_term - normed * scale_term)).astype(
        jnp.bfloat16
    )
    rim_grad = with_rim(grad_conv, half_width)
    input_grad = (depthwise(rim_grad[:, 1:], conv_weight[::-1], frames) * valid).astype(
        jnp.bfloat16
    )
    weight_grad = lax.psum_scatter(
        lax.dot_general(
            flat_active, flat_grad, (((0,), (0,)), ((), ())), preferred_element_type=jnp.float32
        ),
        ("dp", "seq"),
        scatter_dimension=0,
        tiled=True,
    )
    return (output, weight_grad, input_grad)


MESH = pl.DeviceIdType.MESH
LANE = 128


def tile(c):
    return pl.ds(pl.multiple_of(c * LANE, LANE), LANE)


def fused(
    lang_ref, len_ref, x_hbm, tap_hbm, gain_hbm, bias_hbm, w_hbm, cot_hbm,
    out_ref, wg_ref, ig_ref,
    tap_ref, gain_ref, bias_ref, wgrp, cotg, act, act_t, ag, acts, back_t, back_out,
    opart, oin, osum, osend, ox, part, ysum, yin, zin,
    ext, xf, normed, slope, gext,
    info, info_in, stat, stat_in, stat_mid, stat_dp, stat_res,
    local, send, recv,
):
    frames, channels = x_hbm.shape
    taps = tap_ref.shape[0]
    half = taps // 2
    chunks = channels // LANE
    dp, seq = lax.axis_index("dp"), lax.axis_index("seq")
    y, c, z, x = dp // 2, dp % 2, seq // 2, seq % 2
    seq_x, dp_c, dp_y = seq + 1 - 2 * x, dp + 1 - 2 * c, dp + 2 - 4 * y
    to_x, to_c, to_y, to_cx = (dp, seq_x), (dp_c, seq), (dp_y, seq), (dp_c, seq_x)
    xn, cn, yn = 1 - x, 1 - c, 1 - y
    seq_peers = [(dp, (seq + d) % 8) for d in range(1, 8)]
    dp_peers = [((dp + d) % 4, seq) for d in range(1, 4)]
    z_peers = [(z + d) % 4 for d in range(1, 4)]
    lang, length = lang_ref[0], len_ref[0]

    barrier = pltpu.get_barrier_semaphore()
    greet = seq_peers + dp_peers + [to_cx]
    for peer in greet:
        pl.semaphore_signal(barrier, inc=1, device_id=peer, device_id_type=MESH)

    own = [
        pltpu.make_async_copy(src, dst, local.at[i])
        for i, (src, dst) in enumerate((
            (x_hbm, ext.at[half : half + frames]),
            (w_hbm, wgrp.at[y, z]),
            (cot_hbm, cotg.at[0]),
            (tap_hbm, tap_ref),
            (gain_hbm, gain_ref),
            (bias_hbm, bias_ref),
        ))
    ]
    for copy in own:
        copy.start()
    info[0:8, :] = jnp.full((8, LANE), lang, jnp.int32)
    info[8:16, :] = jnp.full((8, LANE), length, jnp.int32)
    for copy in own:
        copy.wait()
    pl.semaphore_wait(barrier, len(greet))

    pending = []
    count = [0]

    def push(src, dst, peer):
        i = count[0]
        count[0] += 1
        copy = pltpu.make_async_remote_copy(
            src_ref=src, dst_ref=dst, send_sem=send.at[i], recv_sem=recv.at[i],
            device_id=peer, device_id_type=MESH,
        )
        copy.start()
        pending.append(copy)
        return copy

    seq_up, seq_down = (dp, (seq + 1) % 8), (dp, (seq + 7) % 8)
    halo = [
        push(ext.at[frames : frames + half], ext.at[0:half], seq_up),
        push(ext.at[half : 2 * half], ext.at[half + frames : frames + 2 * half], seq_down),
    ]
    w_z = [push(wgrp.at[y, z], wgrp.at[y, z], (dp, zp * 2 + x)) for zp in z_peers]
    w_y = [push(wgrp.at[y, z], wgrp.at[y, z], to_y)]
    cot_x = push(cotg.at[0], cotg.at[1], to_x)
    cot_c = push(cotg.at[0], cotg.at[2], to_c)
    told = [push(info, info_in.at[d], peer) for d, peer in enumerate(dp_peers)]

    row = lax.broadcasted_iota(jnp.int32, (frames + 2 * half, LANE), 0) + (seq * frames - half)
    inside = (row >= 0) & (row < length)
    valid = inside[half : half + frames].astype(jnp.float32)

    for copy in halo:
        copy.wait_recv()

    def conv_step(i, carry):
        t = tile(i)
        xf[:, t] = jnp.where(inside, ext[:, t].astype(jnp.float32), 0.0)
        weights = tap_ref[:, t]
        total = jnp.zeros((frames, LANE), jnp.float32)
        for k in range(taps):
            total = total + xf[k : k + frames, t] * weights[k : k + 1]
        normed[:, t] = total
        kept = total * valid
        stat[0, pl.ds(i, 1), :] = jnp.sum(kept, axis=0, keepdims=True)
        stat[0, pl.ds(chunks + i, 1), :] = jnp.sum(kept * total, axis=0, keepdims=True)
        return carry

    lax.fori_loop(0, chunks, conv_step, 0)

    def sum_seq(n):
        return [push(stat.at[n], stat_in.at[n, d], peer) for d, peer in enumerate(seq_peers)]

    def sum_dp(n, copies):
        for copy in copies:
            copy.wait_recv()
        total = stat[n]
        for d in range(7):
            total = total + stat_in[n, d]
        stat_mid[n] = total
        return [push(stat_mid.at[n], stat_dp.at[n, d], peer) for d, peer in enumerate(dp_peers)]

    def finish(n, copies):
        for copy in copies:
            copy.wait_recv()
        total = stat_mid[n]
        frames_of = jnp.full((1, LANE), length, jnp.int32).astype(jnp.float32)
        for d in range(3):
            same = (info_in[d, 0:1, :] == lang).astype(jnp.float32)
            total = total + stat_dp[n, d] * same
            frames_of = frames_of + info_in[d, 8:9, :].astype(jnp.float32) * same
        return total / jnp.maximum(frames_of, 1.0)

    first = sum_seq(0)

    first = sum_dp(0, first)
    for d in range(3):
        w_z[d].wait_recv()
        block = wgrp.at[y, (z + 3 - d) % 4]
        w_y.append(push(block, block, to_y))
    cot_x.wait_recv()
    cot_cx = push(cotg.at[1], cotg.at[3], to_c)
    for copy in told:
        copy.wait_recv()
    mean = finish(0, first)
    average = mean[0:chunks]
    variance = mean[chunks : 2 * chunks] - average * average
    stat_res[0, 0:chunks, :] = average
    stat_res[0, chunks : 2 * chunks, :] = lax.rsqrt(variance + epsilon)

    mine = lax.broadcasted_iota(jnp.int32, (LANGS, LANE), 0) == lang

    def act_step(i, carry):
        t = tile(i)
        average = stat_res[0, pl.ds(i, 1), :]
        inverse = stat_res[0, pl.ds(chunks + i, 1), :]
        gain = jnp.sum(jnp.where(mine, gain_ref[:, t], 0.0), axis=0, keepdims=True)
        bias = jnp.sum(jnp.where(mine, bias_ref[:, t], 0.0), axis=0, keepdims=True)
        norm = (normed[:, t] - average) * inverse
        pre = norm * gain + bias
        s = jax.nn.sigmoid(pre)
        normed[:, t] = norm
        slope[:, t] = valid * s * (1.0 + pre * (1.0 - s)) * gain
        act[:, t] = (pre * s * valid).astype(jnp.bfloat16)
        return carry

    lax.fori_loop(0, chunks, act_step, 0)

    group = channels // 4
    rows = wg_ref.shape[0]
    for g in range(4):
        turned = jnp.transpose(act[:, g * group : (g + 1) * group].astype(jnp.float32))
        act_t[g // 2, g % 2] = turned.astype(jnp.bfloat16).reshape(4, 2, rows, frames)

    factors = [
        push(act_t.at[:, cc, :, xx], ag.at[slot], peer)
        for slot, cc, xx, peer in ((1, c, xn, to_x), (2, cn, x, to_c), (3, cn, xn, to_cx))
    ]
    ag[0] = act_t[:, c, :, x]

    cot_c.wait_recv()
    cot_cx.wait_recv()
    for copy in factors:
        copy.wait_recv()
    lhs = jnp.concatenate([ag[s].reshape(8 * rows, frames) for s in range(4)], axis=1)
    rhs = cotg.reshape(4 * frames, channels)

    def grad_step(i, carry):
        t = pl.ds(pl.multiple_of(i * 256, 256), 256)
        value = jnp.dot(lhs, rhs[:, t], preferred_element_type=jnp.float32)
        part[:, :, :, t] = value.astype(jnp.bfloat16).reshape(2, 4, rows, 256)
        return carry

    lax.fori_loop(0, channels // 256, grad_step, 0)
    order = z_peers + [z]
    over_y = [
        push(part.at[yn, zp], yin.at[d], to_y) for d, zp in enumerate(order)
    ]

    for copy in w_y:
        copy.wait_recv()
    weight = wgrp.reshape(8 * rows, channels)
    where = ((0, c, x, None), (1, c, xn, to_x), (2, cn, x, to_c), (3, cn, xn, to_cx))
    backs = []
    for slot, cc, xx, peer in where:
        value = lax.dot_general(
            weight[...], cotg[slot], (((1,), (1,)), ((), ())),
            preferred_element_type=jnp.float32,
        ).astype(jnp.bfloat16).reshape(2, 4, rows, frames)
        if peer is None:
            back_t[:, c, :, x] = value
        else:
            back_out[slot - 1] = value
            backs.append(push(back_out.at[slot - 1], back_t.at[:, c, :, x], peer))

    acts[...] = jnp.transpose(lhs.astype(jnp.float32)).astype(jnp.bfloat16)

    def out_step(i, carry):
        t = pl.ds(pl.multiple_of(i * 256, 256), 256)
        value = jnp.dot(acts[...], weight[:, t], preferred_element_type=jnp.float32)
        opart[:, :, t] = value.astype(jnp.bfloat16).reshape(4, frames, 256)
        return carry

    lax.fori_loop(0, channels // 256, out_step, 0)
    out_c = push(opart.at[2:4], oin, to_c)

    for copy in backs:
        copy.wait_recv()
    for g in range(4):
        t = slice(g * group, (g + 1) * group)
        piece = back_t[g // 2, g % 2].reshape(group, frames).astype(jnp.float32)
        grad = jnp.transpose(piece) * slope[:, t]
        slope[:, t] = grad
        one = jnp.sum(grad, axis=0, keepdims=True)
        two = jnp.sum(grad * normed[:, t], axis=0, keepdims=True)
        for j in range(group // LANE):
            cut = slice(j * LANE, (j + 1) * LANE)
            at = g * (group // LANE) + j
            stat[1, at : at + 1, :] = one[:, cut]
            stat[1, chunks + at : chunks + at + 1, :] = two[:, cut]
    second = sum_seq(1)

    out_c.wait_recv()
    osend[...] = (opart[1].astype(jnp.float32) + oin[1].astype(jnp.float32)).astype(jnp.bfloat16)
    out_x = push(osend, ox, to_x)
    osum[...] = opart[0].astype(jnp.float32) + oin[0].astype(jnp.float32)

    over_z = []

    def pass_on(d):
        over_y[d].wait_recv()
        added = part[y, order[d]].astype(jnp.float32) + yin[d].astype(jnp.float32)
        if d < 3:
            ysum[d] = added.astype(jnp.bfloat16)
            over_z.append(push(ysum.at[d], zin.at[d], (dp, order[d] * 2 + x)))
        else:
            wg_ref[...] = added

    pass_on(0)
    second = sum_dp(1, second)
    pass_on(1)
    stat_res[1] = finish(1, second)

    def grad_conv_step(i, carry):
        t = tile(i)
        inverse = stat_res[0, pl.ds(chunks + i, 1), :]
        shift = stat_res[1, pl.ds(i, 1), :]
        scale = stat_res[1, pl.ds(chunks + i, 1), :]
        grad = valid * inverse * (slope[:, t] - shift - normed[:, t] * scale)
        gext[half : half + frames, t] = grad.astype(jnp.bfloat16)
        return carry

    lax.fori_loop(0, chunks, grad_conv_step, 0)
    halo = [
        push(gext.at[frames : frames + half], gext.at[0:half], seq_up),
        push(gext.at[half : 2 * half], gext.at[half + frames : frames + 2 * half], seq_down),
    ]
    pass_on(2)
    pass_on(3)
    for copy in halo:
        copy.wait_recv()

    def input_step(i, carry):
        t = tile(i)
        xf[:, t] = jnp.where(inside, gext[:, t].astype(jnp.float32), 0.0)
        weights = tap_ref[:, t]
        total = jnp.zeros((frames, LANE), jnp.float32)
        for k in range(taps):
            total = total + xf[2 * half - k : 2 * half - k + frames, t] * weights[k : k + 1]
        ig_ref[:, t] = (total * valid).astype(jnp.bfloat16)
        return carry

    lax.fori_loop(0, chunks, input_step, 0)
    out_x.wait_recv()
    out_ref[...] = (osum[...] + ox[...].astype(jnp.float32)).astype(jnp.bfloat16)
    total = wg_ref[...]
    for d, copy in enumerate(over_z):
        copy.wait_recv()
        total = total + zin[d].astype(jnp.float32)
    wg_ref[...] = total
    for copy in pending:
        copy.wait_send()


COPIES = 64


def on_device_fused(glu_out, conv_weight, bn_gain, bn_bias, w_out, cotangent, language, length):
    _, frames, channels = glu_out.shape
    rows = w_out.shape[0]
    half = conv_weight.shape[0] // 2
    bf16, f32 = jnp.bfloat16, jnp.float32
    stats = 2 * channels // LANE
    vmem = pl.BlockSpec(memory_space=pltpu.VMEM)
    smem = pl.BlockSpec(memory_space=pltpu.SMEM)
    block_out, weight_grad, input_grad = pl.pallas_call(
        fused,
        out_shape=(
            jax.ShapeDtypeStruct((frames, channels), bf16),
            jax.ShapeDtypeStruct((rows, channels), f32),
            jax.ShapeDtypeStruct((frames, channels), bf16),
        ),
        in_specs=[smem, smem] + [pl.BlockSpec(memory_space=pltpu.HBM)] * 6,
        out_specs=(vmem, vmem, vmem),
        scratch_shapes=[
            pltpu.VMEM(conv_weight.shape, f32),
            pltpu.VMEM(bn_gain.shape, f32),
            pltpu.VMEM(bn_bias.shape, f32),
            pltpu.VMEM((2, 4, rows, channels), bf16),
            pltpu.VMEM((4, frames, channels), bf16),
            pltpu.VMEM((frames, channels), bf16),
            pltpu.VMEM((2, 2, 4, 2, rows, frames), bf16),
            pltpu.VMEM((4, 2, 4, rows, frames), bf16),
            pltpu.VMEM((4 * frames, channels // 4), bf16),
            pltpu.VMEM((2, 2, 4, 2, rows, frames), bf16),
            pltpu.VMEM((3, 2, 4, rows, frames), bf16),
            pltpu.VMEM((4, frames, channels), bf16),
            pltpu.VMEM((2, frames, channels), bf16),
            pltpu.VMEM((frames, channels), f32),
            pltpu.VMEM((frames, channels), bf16),
            pltpu.VMEM((frames, channels), bf16),
            pltpu.VMEM((2, 4, rows, channels), bf16),
            pltpu.VMEM((3, rows, channels), bf16),
            pltpu.VMEM((4, rows, channels), bf16),
            pltpu.VMEM((3, rows, channels), bf16),
            pltpu.VMEM((frames + 2 * half, channels), bf16),
            pltpu.VMEM((frames + 2 * half, channels), f32),
            pltpu.VMEM((frames, channels), f32),
            pltpu.VMEM((frames, channels), f32),
            pltpu.VMEM((frames + 2 * half, channels), bf16),
            pltpu.VMEM((16, LANE), jnp.int32),
            pltpu.VMEM((3, 16, LANE), jnp.int32),
            pltpu.VMEM((2, stats, LANE), f32),
            pltpu.VMEM((2, 7, stats, LANE), f32),
            pltpu.VMEM((2, stats, LANE), f32),
            pltpu.VMEM((2, 3, stats, LANE), f32),
            pltpu.VMEM((2, stats, LANE), f32),
            pltpu.SemaphoreType.DMA((6,)),
            pltpu.SemaphoreType.DMA((COPIES,)),
            pltpu.SemaphoreType.DMA((COPIES,)),
        ],
        compiler_params=pltpu.CompilerParams(
            collective_id=0, has_side_effects=True, vmem_limit_bytes=62 * 1024 * 1024
        ),
    )(language, length, glu_out[0], conv_weight, bn_gain, bn_bias, w_out, cotangent[0])
    return block_out[None], weight_grad, input_grad[None]


def solution(mesh):
    placed = (
        P("dp", "seq", None),
        P(),
        P(),
        P(),
        P(("dp", "seq"), None),
        P("dp", "seq", None),
        P("dp"),
        P("dp"),
    )
    small = mesh.shape["dp"] == 4 and mesh.shape["seq"] == 8
    return jax.shard_map(
        on_device_fused if small else on_device,
        mesh=mesh,
        in_specs=placed,
        out_specs=(P("dp", "seq", None), P(("dp", "seq"), None), P("dp", "seq", None)),
        check_vma=False,
    )
```

```python
import jax
import jax.numpy as jnp
from jax import lax
from jax.experimental import pallas as pl
from jax.experimental.pallas import tpu as pltpu
from jax.sharding import PartitionSpec as P

LANGS = 16


epsilon = 1e-05


def with_halo(array, sides, width):
    for axis, dim in sides:
        size, length = (lax.axis_size(axis), array.shape[dim])
        up = [(i, (i + 1) % size) for i in range(size - 1)]
        down = [(j, i) for i, j in up]
        last = lax.slice_in_dim(array, length - width, length, axis=dim)
        first = lax.slice_in_dim(array, 0, width, axis=dim)
        before = lax.ppermute(last, axis, up)
        after = lax.ppermute(first, axis, down)
        array = jnp.concatenate([before, array, after], axis=dim)
    return array


def depthwise(padded, taps, frames):
    running = jnp.zeros((padded.shape[0], frames, padded.shape[2]), jnp.float32)
    for offset in range(taps.shape[0]):
        running = running + padded[:, offset : offset + frames].astype(jnp.float32) * taps[offset]
    return running


def with_rim(values, half_width):
    return with_halo(values, (("seq", 1),), half_width)


def per_language(one_hot, values_table):
    return jnp.dot(one_hot.T, values_table, precision=lax.Precision.HIGHEST)


def per_utterance(one_hot, values_table):
    return jnp.dot(one_hot, values_table, precision=lax.Precision.HIGHEST)[:, None, :]


def on_device(glu_out, conv_weight, bn_gain, bn_bias, w_out, cotangent, language, length):
    utterances, frames, channels = glu_out.shape
    kernel = conv_weight.shape[0]
    half_width = kernel // 2
    position = lax.axis_index("seq") * frames + lax.iota(jnp.int32, frames)
    valid = (position[None, :] < length[:, None]).astype(jnp.float32)[:, :, None]
    one_hot = (language[:, None] == lax.iota(jnp.int32, LANGS)[None, :]).astype(jnp.float32)
    masked = glu_out * valid.astype(jnp.bfloat16)
    extended = with_rim(masked, half_width)
    convolved = depthwise(extended[:, : frames + kernel - 1], conv_weight, frames)
    counts = per_language(one_hot, jnp.sum(valid, axis=(1, 2)))
    local_sum = per_language(one_hot, jnp.sum(convolved * valid, axis=1))
    local_square = per_language(one_hot, jnp.sum(convolved * convolved * valid, axis=1))
    total_sum, total_square, total_count = lax.psum(
        (local_sum, local_square, counts), ("dp", "seq")
    )
    denominator = jnp.maximum(total_count, 1.0)[:, None]
    average = total_sum / denominator
    variance = total_square / denominator - average * average
    average_utt = per_utterance(one_hot, average)
    inverse_utt = per_utterance(one_hot, lax.rsqrt(variance + epsilon))
    gain_utt = per_utterance(one_hot, bn_gain)
    bias_utt = per_utterance(one_hot, bn_bias)
    normed = (convolved - average_utt) * inverse_utt
    pre_act = normed * gain_utt + bias_utt
    sigmoid_act = jax.nn.sigmoid(pre_act)
    active = (pre_act * sigmoid_act * valid).astype(jnp.bfloat16)
    full_weight = lax.all_gather(w_out, ("dp", "seq"), axis=0, tiled=True)
    flat_active = active.reshape(utterances * frames, channels)
    flat_grad = cotangent.reshape(utterances * frames, channels)
    output = jnp.dot(flat_active, full_weight, preferred_element_type=jnp.float32)
    output = output.astype(jnp.bfloat16).reshape(utterances, frames, channels)
    back_proj = lax.dot_general(
        flat_grad, full_weight, (((1,), (1,)), ((), ())), preferred_element_type=jnp.float32
    )
    back_proj = back_proj.reshape(utterances, frames, channels)
    grad_pre = back_proj * valid * sigmoid_act * (1.0 + pre_act * (1.0 - sigmoid_act))
    grad_normed = grad_pre * gain_utt
    first_sum, second_sum = lax.psum(
        (
            per_language(one_hot, jnp.sum(grad_normed, axis=1)),
            per_language(one_hot, jnp.sum(grad_normed * normed, axis=1)),
        ),
        ("dp", "seq"),
    )
    shift_term = per_utterance(one_hot, first_sum / denominator)
    scale_term = per_utterance(one_hot, second_sum / denominator)
    grad_conv = (valid * inverse_utt * (grad_normed - shift_term - normed * scale_term)).astype(
        jnp.bfloat16
    )
    rim_grad = with_rim(grad_conv, half_width)
    input_grad = (depthwise(rim_grad[:, 1:], conv_weight[::-1], frames) * valid).astype(
        jnp.bfloat16
    )
    weight_grad = lax.psum_scatter(
        lax.dot_general(
            flat_active, flat_grad, (((0,), (0,)), ((), ())), preferred_element_type=jnp.float32
        ),
        ("dp", "seq"),
        scatter_dimension=0,
        tiled=True,
    )
    return (output, weight_grad, input_grad)


MESH = pl.DeviceIdType.MESH
LANE = 128


def tile(c):
    return pl.ds(pl.multiple_of(c * LANE, LANE), LANE)


def fused(
    lang_ref, len_ref, x_hbm, tap_hbm, gain_hbm, bias_hbm, w_hbm, cot_hbm,
    out_hbm, wg_hbm, ig_hbm,
    out_ref, wg_ref, ig_ref,
    tap_ref, gain_ref, bias_ref, wgrp, cotg, act, act_t, ag, acts, back_t, back_out,
    opart, oin, osum, osend, ox, part, ysum, yin, zin,
    ext, xf, normed, slope, gext,
    info, info_in, stat, stat_in, stat_mid, stat_dp, stat_res,
    local, send, recv,
):
    frames, channels = x_hbm.shape
    taps = tap_ref.shape[0]
    half = taps // 2
    chunks = channels // LANE
    dp, seq = lax.axis_index("dp"), lax.axis_index("seq")
    y, c, z, x = dp // 2, dp % 2, seq // 2, seq % 2
    seq_x, dp_c, dp_y = seq + 1 - 2 * x, dp + 1 - 2 * c, dp + 2 - 4 * y
    to_x, to_c, to_y, to_cx = (dp, seq_x), (dp_c, seq), (dp_y, seq), (dp_c, seq_x)
    xn, cn, yn = 1 - x, 1 - c, 1 - y
    seq_peers = [(dp, (seq + d) % 8) for d in range(1, 8)]
    dp_peers = [((dp + d) % 4, seq) for d in range(1, 4)]
    z_peers = [(z + d) % 4 for d in range(1, 4)]
    lang, length = lang_ref[0], len_ref[0]

    barrier = pltpu.get_barrier_semaphore()
    greet = seq_peers + dp_peers + [to_cx]
    for peer in greet:
        pl.semaphore_signal(barrier, inc=1, device_id=peer, device_id_type=MESH)

    own = [
        pltpu.make_async_copy(src, dst, local.at[i])
        for i, (src, dst) in enumerate((
            (x_hbm, ext.at[half : half + frames]),
            (w_hbm, wgrp.at[y, z]),
            (cot_hbm, cotg.at[0]),
            (tap_hbm, tap_ref),
            (gain_hbm, gain_ref),
            (bias_hbm, bias_ref),
        ))
    ]
    for copy in own:
        copy.start()
    info[0:8, :] = jnp.full((8, LANE), lang, jnp.int32)
    info[8:16, :] = jnp.full((8, LANE), length, jnp.int32)
    for copy in own:
        copy.wait()
    pl.semaphore_wait(barrier, len(greet))

    pending = []
    count = [0]

    def push(src, dst, peer):
        i = count[0]
        count[0] += 1
        copy = pltpu.make_async_remote_copy(
            src_ref=src, dst_ref=dst, send_sem=send.at[i], recv_sem=recv.at[i],
            device_id=peer, device_id_type=MESH,
        )
        copy.start()
        pending.append(copy)
        return copy

    seq_up, seq_down = (dp, (seq + 1) % 8), (dp, (seq + 7) % 8)
    halo = [
        push(ext.at[frames : frames + half], ext.at[0:half], seq_up),
        push(ext.at[half : 2 * half], ext.at[half + frames : frames + 2 * half], seq_down),
    ]
    w_z = [push(wgrp.at[y, z], wgrp.at[y, z], (dp, zp * 2 + x)) for zp in z_peers]
    w_y = [push(wgrp.at[y, z], wgrp.at[y, z], to_y)]
    cot_x = push(cotg.at[0], cotg.at[1], to_x)
    cot_c = push(cotg.at[0], cotg.at[2], to_c)
    told = [push(info, info_in.at[d], peer) for d, peer in enumerate(dp_peers)]

    row = lax.broadcasted_iota(jnp.int32, (frames + 2 * half, LANE), 0) + (seq * frames - half)
    inside = (row >= 0) & (row < length)
    valid = inside[half : half + frames].astype(jnp.float32)

    for copy in halo:
        copy.wait_recv()

    def conv_step(i, carry):
        t = tile(i)
        xf[:, t] = jnp.where(inside, ext[:, t].astype(jnp.float32), 0.0)
        weights = tap_ref[:, t]
        total = jnp.zeros((frames, LANE), jnp.float32)
        for k in range(taps):
            total = total + xf[k : k + frames, t] * weights[k : k + 1]
        normed[:, t] = total
        kept = total * valid
        stat[0, pl.ds(i, 1), :] = jnp.sum(kept, axis=0, keepdims=True)
        stat[0, pl.ds(chunks + i, 1), :] = jnp.sum(kept * total, axis=0, keepdims=True)
        return carry

    lax.fori_loop(0, chunks, conv_step, 0)

    def sum_seq(n):
        return [push(stat.at[n], stat_in.at[n, d], peer) for d, peer in enumerate(seq_peers)]

    def sum_dp(n, copies):
        for copy in copies:
            copy.wait_recv()
        total = stat[n]
        for d in range(7):
            total = total + stat_in[n, d]
        stat_mid[n] = total
        return [push(stat_mid.at[n], stat_dp.at[n, d], peer) for d, peer in enumerate(dp_peers)]

    def finish(n, copies):
        for copy in copies:
            copy.wait_recv()
        total = stat_mid[n]
        frames_of = jnp.full((1, LANE), length, jnp.int32).astype(jnp.float32)
        for d in range(3):
            same = (info_in[d, 0:1, :] == lang).astype(jnp.float32)
            total = total + stat_dp[n, d] * same
            frames_of = frames_of + info_in[d, 8:9, :].astype(jnp.float32) * same
        return total / jnp.maximum(frames_of, 1.0)

    first = sum_seq(0)

    first = sum_dp(0, first)
    for d in range(3):
        w_z[d].wait_recv()
        block = wgrp.at[y, (z + 3 - d) % 4]
        w_y.append(push(block, block, to_y))
    cot_x.wait_recv()
    cot_cx = push(cotg.at[1], cotg.at[3], to_c)
    for copy in told:
        copy.wait_recv()
    mean = finish(0, first)
    average = mean[0:chunks]
    variance = mean[chunks : 2 * chunks] - average * average
    stat_res[0, 0:chunks, :] = average
    stat_res[0, chunks : 2 * chunks, :] = lax.rsqrt(variance + epsilon)

    mine = lax.broadcasted_iota(jnp.int32, (LANGS, LANE), 0) == lang

    def act_step(i, carry):
        t = tile(i)
        average = stat_res[0, pl.ds(i, 1), :]
        inverse = stat_res[0, pl.ds(chunks + i, 1), :]
        gain = jnp.sum(jnp.where(mine, gain_ref[:, t], 0.0), axis=0, keepdims=True)
        bias = jnp.sum(jnp.where(mine, bias_ref[:, t], 0.0), axis=0, keepdims=True)
        norm = (normed[:, t] - average) * inverse
        pre = norm * gain + bias
        s = jax.nn.sigmoid(pre)
        normed[:, t] = norm
        slope[:, t] = valid * s * (1.0 + pre * (1.0 - s)) * gain
        act[:, t] = (pre * s * valid).astype(jnp.bfloat16)
        return carry

    lax.fori_loop(0, chunks, act_step, 0)

    group = channels // 4
    rows = wg_ref.shape[0]
    for g in range(4):
        turned = jnp.transpose(act[:, g * group : (g + 1) * group].astype(jnp.float32))
        act_t[g // 2, g % 2] = turned.astype(jnp.bfloat16).reshape(4, 2, rows, frames)

    factors = [
        push(act_t.at[:, cc, :, xx], ag.at[slot], peer)
        for slot, cc, xx, peer in ((1, c, xn, to_x), (2, cn, x, to_c), (3, cn, xn, to_cx))
    ]
    ag[0] = act_t[:, c, :, x]

    cot_c.wait_recv()
    cot_cx.wait_recv()
    for copy in factors:
        copy.wait_recv()
    lhs = jnp.concatenate([ag[s].reshape(8 * rows, frames) for s in range(4)], axis=1)
    rhs = cotg.reshape(4 * frames, channels)

    def grad_step(i, carry):
        t = pl.ds(pl.multiple_of(i * 256, 256), 256)
        value = jnp.dot(lhs, rhs[:, t], preferred_element_type=jnp.float32)
        part[:, :, :, t] = value.astype(jnp.bfloat16).reshape(2, 4, rows, 256)
        return carry

    lax.fori_loop(0, channels // 256, grad_step, 0)
    order = z_peers + [z]
    over_y = [
        push(part.at[yn, zp], yin.at[d], to_y) for d, zp in enumerate(order)
    ]

    for copy in w_y:
        copy.wait_recv()
    weight = wgrp.reshape(8 * rows, channels)
    where = ((0, c, x, None), (1, c, xn, to_x), (2, cn, x, to_c), (3, cn, xn, to_cx))
    backs = []
    for slot, cc, xx, peer in where:
        value = lax.dot_general(
            weight[...], cotg[slot], (((1,), (1,)), ((), ())),
            preferred_element_type=jnp.float32,
        ).astype(jnp.bfloat16).reshape(2, 4, rows, frames)
        if peer is None:
            back_t[:, c, :, x] = value
        else:
            back_out[slot - 1] = value
            backs.append(push(back_out.at[slot - 1], back_t.at[:, c, :, x], peer))

    acts[...] = jnp.transpose(lhs.astype(jnp.float32)).astype(jnp.bfloat16)

    def out_step(i, carry):
        t = pl.ds(pl.multiple_of(i * 256, 256), 256)
        value = jnp.dot(acts[...], weight[:, t], preferred_element_type=jnp.float32)
        opart[:, :, t] = value.astype(jnp.bfloat16).reshape(4, frames, 256)
        return carry

    lax.fori_loop(0, channels // 256, out_step, 0)
    out_c = push(opart.at[2:4], oin, to_c)

    over_z = []

    def pass_on(d):
        over_y[d].wait_recv()
        added = part[y, order[d]].astype(jnp.float32) + yin[d].astype(jnp.float32)
        if d < 3:
            ysum[d] = added.astype(jnp.bfloat16)
            over_z.append(push(ysum.at[d], zin.at[d], (dp, order[d] * 2 + x)))
        else:
            wg_ref[...] = added

    pass_on(0)

    for copy in backs:
        copy.wait_recv()
    for g in range(4):
        t = slice(g * group, (g + 1) * group)
        piece = back_t[g // 2, g % 2].reshape(group, frames).astype(jnp.float32)
        grad = jnp.transpose(piece) * slope[:, t]
        slope[:, t] = grad
        one = jnp.sum(grad, axis=0, keepdims=True)
        two = jnp.sum(grad * normed[:, t], axis=0, keepdims=True)
        for j in range(group // LANE):
            cut = slice(j * LANE, (j + 1) * LANE)
            at = g * (group // LANE) + j
            stat[1, at : at + 1, :] = one[:, cut]
            stat[1, chunks + at : chunks + at + 1, :] = two[:, cut]
    second = sum_seq(1)

    out_c.wait_recv()
    osend[...] = (opart[1].astype(jnp.float32) + oin[1].astype(jnp.float32)).astype(jnp.bfloat16)
    out_x = push(osend, ox, to_x)
    osum[...] = opart[0].astype(jnp.float32) + oin[0].astype(jnp.float32)

    pass_on(1)
    second = sum_dp(1, second)
    pass_on(2)
    stat_res[1] = finish(1, second)

    def grad_conv_step(i, carry):
        t = tile(i)
        inverse = stat_res[0, pl.ds(chunks + i, 1), :]
        shift = stat_res[1, pl.ds(i, 1), :]
        scale = stat_res[1, pl.ds(chunks + i, 1), :]
        grad = valid * inverse * (slope[:, t] - shift - normed[:, t] * scale)
        gext[half : half + frames, t] = grad.astype(jnp.bfloat16)
        return carry

    lax.fori_loop(0, chunks, grad_conv_step, 0)
    halo = [
        push(gext.at[frames : frames + half], gext.at[0:half], seq_up),
        push(gext.at[half : 2 * half], gext.at[half + frames : frames + 2 * half], seq_down),
    ]
    pass_on(3)
    out_x.wait_recv()
    out_ref[...] = (osum[...] + ox[...].astype(jnp.float32)).astype(jnp.bfloat16)
    leave = [pltpu.make_async_copy(out_ref, out_hbm, local.at[0])]
    leave[0].start()
    for copy in halo:
        copy.wait_recv()

    def input_step(i, carry):
        t = tile(i)
        xf[:, t] = jnp.where(inside, gext[:, t].astype(jnp.float32), 0.0)
        weights = tap_ref[:, t]
        total = jnp.zeros((frames, LANE), jnp.float32)
        for k in range(taps):
            total = total + xf[2 * half - k : 2 * half - k + frames, t] * weights[k : k + 1]
        ig_ref[:, t] = (total * valid).astype(jnp.bfloat16)
        return carry

    for g in range(4):
        lax.fori_loop(g * chunks // 4, (g + 1) * chunks // 4, input_step, 0)
        t = pl.ds(g * group, group)
        leave.append(pltpu.make_async_copy(ig_ref.at[:, t], ig_hbm.at[:, t], local.at[1 + g]))
        leave[-1].start()
    total = wg_ref[...]
    for d, copy in enumerate(over_z):
        copy.wait_recv()
        total = total + zin[d].astype(jnp.float32)
    wg_ref[...] = total
    leave.append(pltpu.make_async_copy(wg_ref, wg_hbm, local.at[5]))
    leave[-1].start()
    for copy in leave:
        copy.wait()
    for copy in pending:
        copy.wait_send()


COPIES = 64


def hand_over(a_in, b_in, c_in, a_out, b_out, c_out, sems):
    copies = []
    for src, dst in ((a_in, a_out), (b_in, b_out), (c_in, c_out)):
        step = src.shape[0] // 3 if src.shape[0] % 48 == 0 else src.shape[0] // 4
        for at in range(0, src.shape[0], step):
            cut = pl.ds(at, step)
            copies.append(pltpu.make_async_copy(src.at[cut], dst.at[cut], sems.at[len(copies)]))
    for copy in copies:
        copy.start()
    for copy in copies:
        copy.wait()


def on_device_fused(glu_out, conv_weight, bn_gain, bn_bias, w_out, cotangent, language, length):
    _, frames, channels = glu_out.shape
    rows = w_out.shape[0]
    half = conv_weight.shape[0] // 2
    bf16, f32 = jnp.bfloat16, jnp.float32
    stats = 2 * channels // LANE
    hbm = pl.BlockSpec(memory_space=pltpu.HBM)
    smem = pl.BlockSpec(memory_space=pltpu.SMEM)
    results = (
        jax.ShapeDtypeStruct((frames, channels), bf16),
        jax.ShapeDtypeStruct((rows, channels), f32),
        jax.ShapeDtypeStruct((frames, channels), bf16),
    )
    made = pl.pallas_call(
        fused,
        out_shape=results,
        in_specs=[smem, smem] + [hbm] * 6,
        out_specs=(hbm, hbm, hbm),
        scratch_shapes=[
            pltpu.VMEM((frames, channels), bf16),
            pltpu.VMEM((rows, channels), f32),
            pltpu.VMEM((frames, channels), bf16),
            pltpu.VMEM(conv_weight.shape, f32),
            pltpu.VMEM(bn_gain.shape, f32),
            pltpu.VMEM(bn_bias.shape, f32),
            pltpu.VMEM((2, 4, rows, channels), bf16),
            pltpu.VMEM((4, frames, channels), bf16),
            pltpu.VMEM((frames, channels), bf16),
            pltpu.VMEM((2, 2, 4, 2, rows, frames), bf16),
            pltpu.VMEM((4, 2, 4, rows, frames), bf16),
            pltpu.VMEM((4 * frames, channels // 4), bf16),
            pltpu.VMEM((2, 2, 4, 2, rows, frames), bf16),
            pltpu.VMEM((3, 2, 4, rows, frames), bf16),
            pltpu.VMEM((4, frames, channels), bf16),
            pltpu.VMEM((2, frames, channels), bf16),
            pltpu.VMEM((frames, channels), f32),
            pltpu.VMEM((frames, channels), bf16),
            pltpu.VMEM((frames, channels), bf16),
            pltpu.VMEM((2, 4, rows, channels), bf16),
            pltpu.VMEM((3, rows, channels), bf16),
            pltpu.VMEM((4, rows, channels), bf16),
            pltpu.VMEM((3, rows, channels), bf16),
            pltpu.VMEM((frames + 2 * half, channels), bf16),
            pltpu.VMEM((frames + 2 * half, channels), f32),
            pltpu.VMEM((frames, channels), f32),
            pltpu.VMEM((frames, channels), f32),
            pltpu.VMEM((frames + 2 * half, channels), bf16),
            pltpu.VMEM((16, LANE), jnp.int32),
            pltpu.VMEM((3, 16, LANE), jnp.int32),
            pltpu.VMEM((2, stats, LANE), f32),
            pltpu.VMEM((2, 7, stats, LANE), f32),
            pltpu.VMEM((2, stats, LANE), f32),
            pltpu.VMEM((2, 3, stats, LANE), f32),
            pltpu.VMEM((2, stats, LANE), f32),
            pltpu.SemaphoreType.DMA((6,)),
            pltpu.SemaphoreType.DMA((COPIES,)),
            pltpu.SemaphoreType.DMA((COPIES,)),
        ],
        compiler_params=pltpu.CompilerParams(
            collective_id=0, has_side_effects=True, vmem_limit_bytes=62 * 1024 * 1024
        ),
    )(language, length, glu_out[0], conv_weight, bn_gain, bn_bias, w_out, cotangent[0])
    block_out, weight_grad, input_grad = pl.pallas_call(
        hand_over,
        out_shape=results,
        in_specs=[hbm] * 3,
        out_specs=(hbm, hbm, hbm),
        scratch_shapes=[pltpu.SemaphoreType.DMA((12,))],
        compiler_params=pltpu.CompilerParams(vmem_limit_bytes=62 * 1024 * 1024),
    )(*made)
    return block_out[None], weight_grad, input_grad[None]


def solution(mesh):
    placed = (
        P("dp", "seq", None),
        P(),
        P(),
        P(),
        P(("dp", "seq"), None),
        P("dp", "seq", None),
        P("dp"),
        P("dp"),
    )
    small = mesh.shape["dp"] == 4 and mesh.shape["seq"] == 8
    return jax.shard_map(
        on_device_fused if small else on_device,
        mesh=mesh,
        in_specs=placed,
        out_specs=(P("dp", "seq", None), P(("dp", "seq"), None), P("dp", "seq", None)),
        check_vma=False,
    )
```

```python
import jax
import jax.numpy as jnp
from jax import lax
from jax.experimental import pallas as pl
from jax.experimental.pallas import tpu as pltpu
from jax.sharding import PartitionSpec as P

LANGS = 16


epsilon = 1e-05


def with_halo(array, sides, width):
    for axis, dim in sides:
        size, length = (lax.axis_size(axis), array.shape[dim])
        up = [(i, (i + 1) % size) for i in range(size - 1)]
        down = [(j, i) for i, j in up]
        last = lax.slice_in_dim(array, length - width, length, axis=dim)
        first = lax.slice_in_dim(array, 0, width, axis=dim)
        before = lax.ppermute(last, axis, up)
        after = lax.ppermute(first, axis, down)
        array = jnp.concatenate([before, array, after], axis=dim)
    return array


def depthwise(padded, taps, frames):
    running = jnp.zeros((padded.shape[0], frames, padded.shape[2]), jnp.float32)
    for offset in range(taps.shape[0]):
        running = running + padded[:, offset : offset + frames].astype(jnp.float32) * taps[offset]
    return running


def with_rim(values, half_width):
    return with_halo(values, (("seq", 1),), half_width)


def per_language(one_hot, values_table):
    return jnp.dot(one_hot.T, values_table, precision=lax.Precision.HIGHEST)


def per_utterance(one_hot, values_table):
    return jnp.dot(one_hot, values_table, precision=lax.Precision.HIGHEST)[:, None, :]


def on_device(glu_out, conv_weight, bn_gain, bn_bias, w_out, cotangent, language, length):
    utterances, frames, channels = glu_out.shape
    kernel = conv_weight.shape[0]
    half_width = kernel // 2
    position = lax.axis_index("seq") * frames + lax.iota(jnp.int32, frames)
    valid = (position[None, :] < length[:, None]).astype(jnp.float32)[:, :, None]
    one_hot = (language[:, None] == lax.iota(jnp.int32, LANGS)[None, :]).astype(jnp.float32)
    masked = glu_out * valid.astype(jnp.bfloat16)
    extended = with_rim(masked, half_width)
    convolved = depthwise(extended[:, : frames + kernel - 1], conv_weight, frames)
    counts = per_language(one_hot, jnp.sum(valid, axis=(1, 2)))
    local_sum = per_language(one_hot, jnp.sum(convolved * valid, axis=1))
    local_square = per_language(one_hot, jnp.sum(convolved * convolved * valid, axis=1))
    total_sum, total_square, total_count = lax.psum(
        (local_sum, local_square, counts), ("dp", "seq")
    )
    denominator = jnp.maximum(total_count, 1.0)[:, None]
    average = total_sum / denominator
    variance = total_square / denominator - average * average
    average_utt = per_utterance(one_hot, average)
    inverse_utt = per_utterance(one_hot, lax.rsqrt(variance + epsilon))
    gain_utt = per_utterance(one_hot, bn_gain)
    bias_utt = per_utterance(one_hot, bn_bias)
    normed = (convolved - average_utt) * inverse_utt
    pre_act = normed * gain_utt + bias_utt
    sigmoid_act = jax.nn.sigmoid(pre_act)
    active = (pre_act * sigmoid_act * valid).astype(jnp.bfloat16)
    full_weight = lax.all_gather(w_out, ("dp", "seq"), axis=0, tiled=True)
    flat_active = active.reshape(utterances * frames, channels)
    flat_grad = cotangent.reshape(utterances * frames, channels)
    output = jnp.dot(flat_active, full_weight, preferred_element_type=jnp.float32)
    output = output.astype(jnp.bfloat16).reshape(utterances, frames, channels)
    back_proj = lax.dot_general(
        flat_grad, full_weight, (((1,), (1,)), ((), ())), preferred_element_type=jnp.float32
    )
    back_proj = back_proj.reshape(utterances, frames, channels)
    grad_pre = back_proj * valid * sigmoid_act * (1.0 + pre_act * (1.0 - sigmoid_act))
    grad_normed = grad_pre * gain_utt
    first_sum, second_sum = lax.psum(
        (
            per_language(one_hot, jnp.sum(grad_normed, axis=1)),
            per_language(one_hot, jnp.sum(grad_normed * normed, axis=1)),
        ),
        ("dp", "seq"),
    )
    shift_term = per_utterance(one_hot, first_sum / denominator)
    scale_term = per_utterance(one_hot, second_sum / denominator)
    grad_conv = (valid * inverse_utt * (grad_normed - shift_term - normed * scale_term)).astype(
        jnp.bfloat16
    )
    rim_grad = with_rim(grad_conv, half_width)
    input_grad = (depthwise(rim_grad[:, 1:], conv_weight[::-1], frames) * valid).astype(
        jnp.bfloat16
    )
    weight_grad = lax.psum_scatter(
        lax.dot_general(
            flat_active, flat_grad, (((0,), (0,)), ((), ())), preferred_element_type=jnp.float32
        ),
        ("dp", "seq"),
        scatter_dimension=0,
        tiled=True,
    )
    return (output, weight_grad, input_grad)


MESH = pl.DeviceIdType.MESH
LANE = 128


def tile(c):
    return pl.ds(pl.multiple_of(c * LANE, LANE), LANE)


def fused(
    lang_ref, len_ref, x_hbm, tap_hbm, gain_hbm, bias_hbm, w_hbm, cot_hbm,
    out_hbm, wg_hbm, ig_hbm,
    out_ref, wg_ref, ig_ref,
    tap_ref, gain_ref, bias_ref, wgrp, cotg, act, act_t, ag, acts, back_t, back_out,
    opart, oin, osum, osend, ox, part, ysum, yin, zin,
    ext, xf, normed, slope, gext,
    info, info_in, stat, stat_in, stat_mid, stat_dp, stat_res,
    local, send, recv,
):
    frames, channels = x_hbm.shape
    taps = tap_ref.shape[0]
    half = taps // 2
    chunks = channels // LANE
    dp, seq = lax.axis_index("dp"), lax.axis_index("seq")
    y, c, z, x = dp // 2, dp % 2, seq // 2, seq % 2
    seq_x, dp_c, dp_y = seq + 1 - 2 * x, dp + 1 - 2 * c, dp + 2 - 4 * y
    to_x, to_c, to_y, to_cx = (dp, seq_x), (dp_c, seq), (dp_y, seq), (dp_c, seq_x)
    xn, cn, yn = 1 - x, 1 - c, 1 - y
    seq_peers = [(dp, (seq + d) % 8) for d in range(1, 8)]
    dp_peers = [((dp + d) % 4, seq) for d in range(1, 4)]
    z_peers = [(z + d) % 4 for d in range(1, 4)]
    lang, length = lang_ref[0], len_ref[0]

    barrier = pltpu.get_barrier_semaphore()
    greet = seq_peers + dp_peers + [to_cx]
    for peer in greet:
        pl.semaphore_signal(barrier, inc=1, device_id=peer, device_id_type=MESH)

    own = [
        pltpu.make_async_copy(src, dst, local.at[i])
        for i, (src, dst) in enumerate((
            (x_hbm, ext.at[half : half + frames]),
            (w_hbm, wgrp.at[y, z]),
            (cot_hbm, cotg.at[0]),
            (tap_hbm, tap_ref),
            (gain_hbm, gain_ref),
            (bias_hbm, bias_ref),
        ))
    ]
    for copy in own:
        copy.start()
    info[0:8, :] = jnp.full((8, LANE), lang, jnp.int32)
    info[8:16, :] = jnp.full((8, LANE), length, jnp.int32)
    for copy in own:
        copy.wait()
    pl.semaphore_wait(barrier, len(greet))

    pending = []
    count = [0]

    def push(src, dst, peer):
        i = count[0]
        count[0] += 1
        copy = pltpu.make_async_remote_copy(
            src_ref=src, dst_ref=dst, send_sem=send.at[i], recv_sem=recv.at[i],
            device_id=peer, device_id_type=MESH,
        )
        copy.start()
        pending.append(copy)
        return copy

    seq_up, seq_down = (dp, (seq + 1) % 8), (dp, (seq + 7) % 8)
    halo = [
        push(ext.at[frames : frames + half], ext.at[0:half], seq_up),
        push(ext.at[half : 2 * half], ext.at[half + frames : frames + 2 * half], seq_down),
    ]
    w_z = [push(wgrp.at[y, z], wgrp.at[y, z], (dp, zp * 2 + x)) for zp in z_peers]
    w_y = [push(wgrp.at[y, z], wgrp.at[y, z], to_y)]
    cot_x = push(cotg.at[0], cotg.at[1], to_x)
    cot_c = push(cotg.at[0], cotg.at[2], to_c)
    told = [push(info, info_in.at[d], peer) for d, peer in enumerate(dp_peers)]

    row = lax.broadcasted_iota(jnp.int32, (frames + 2 * half, LANE), 0) + (seq * frames - half)
    inside = (row >= 0) & (row < length)
    valid = inside[half : half + frames].astype(jnp.float32)

    for copy in halo:
        copy.wait_recv()

    def conv_step(i, carry):
        t = tile(i)
        xf[:, t] = jnp.where(inside, ext[:, t].astype(jnp.float32), 0.0)
        weights = tap_ref[:, t]
        total = jnp.zeros((frames, LANE), jnp.float32)
        for k in range(taps):
            total = total + xf[k : k + frames, t] * weights[k : k + 1]
        normed[:, t] = total
        kept = total * valid
        stat[0, pl.ds(i, 1), :] = jnp.sum(kept, axis=0, keepdims=True)
        stat[0, pl.ds(chunks + i, 1), :] = jnp.sum(kept * total, axis=0, keepdims=True)
        return carry

    lax.fori_loop(0, chunks, conv_step, 0)

    def sum_seq(n):
        return [push(stat.at[n], stat_in.at[n, d], peer) for d, peer in enumerate(seq_peers)]

    def sum_dp(n, copies):
        for copy in copies:
            copy.wait_recv()
        total = stat[n]
        for d in range(7):
            total = total + stat_in[n, d]
        stat_mid[n] = total
        return [push(stat_mid.at[n], stat_dp.at[n, d], peer) for d, peer in enumerate(dp_peers)]

    def finish(n, copies):
        for copy in copies:
            copy.wait_recv()
        total = stat_mid[n]
        frames_of = jnp.full((1, LANE), length, jnp.int32).astype(jnp.float32)
        for d in range(3):
            same = (info_in[d, 0:1, :] == lang).astype(jnp.float32)
            total = total + stat_dp[n, d] * same
            frames_of = frames_of + info_in[d, 8:9, :].astype(jnp.float32) * same
        return total / jnp.maximum(frames_of, 1.0)

    first = sum_seq(0)

    first = sum_dp(0, first)
    for d in range(3):
        w_z[d].wait_recv()
        block = wgrp.at[y, (z + 3 - d) % 4]
        w_y.append(push(block, block, to_y))
    cot_x.wait_recv()
    cot_cx = push(cotg.at[1], cotg.at[3], to_c)
    for copy in told:
        copy.wait_recv()
    mean = finish(0, first)
    average = mean[0:chunks]
    variance = mean[chunks : 2 * chunks] - average * average
    stat_res[0, 0:chunks, :] = average
    stat_res[0, chunks : 2 * chunks, :] = lax.rsqrt(variance + epsilon)

    mine = lax.broadcasted_iota(jnp.int32, (LANGS, LANE), 0) == lang

    def act_step(i, carry):
        t = tile(i)
        average = stat_res[0, pl.ds(i, 1), :]
        inverse = stat_res[0, pl.ds(chunks + i, 1), :]
        gain = jnp.sum(jnp.where(mine, gain_ref[:, t], 0.0), axis=0, keepdims=True)
        bias = jnp.sum(jnp.where(mine, bias_ref[:, t], 0.0), axis=0, keepdims=True)
        norm = (normed[:, t] - average) * inverse
        pre = norm * gain + bias
        s = jax.nn.sigmoid(pre)
        normed[:, t] = norm
        slope[:, t] = valid * s * (1.0 + pre * (1.0 - s)) * gain
        act[:, t] = (pre * s * valid).astype(jnp.bfloat16)
        return carry

    lax.fori_loop(0, chunks, act_step, 0)

    group = channels // 4
    rows = wg_ref.shape[0]
    for g in range(4):
        turned = jnp.transpose(act[:, g * group : (g + 1) * group].astype(jnp.float32))
        act_t[g // 2, g % 2] = turned.astype(jnp.bfloat16).reshape(4, 2, rows, frames)

    factors = [
        push(act_t.at[:, cc, :, xx], ag.at[slot], peer)
        for slot, cc, xx, peer in ((1, c, xn, to_x), (2, cn, x, to_c), (3, cn, xn, to_cx))
    ]
    ag[0] = act_t[:, c, :, x]

    cot_c.wait_recv()
    cot_cx.wait_recv()
    for copy in factors:
        copy.wait_recv()
    lhs = jnp.concatenate([ag[s].reshape(8 * rows, frames) for s in range(4)], axis=1)
    rhs = cotg.reshape(4 * frames, channels)

    def grad_step(i, carry):
        t = pl.ds(pl.multiple_of(i * 256, 256), 256)
        value = jnp.dot(lhs, rhs[:, t], preferred_element_type=jnp.float32)
        part[:, :, :, t] = value.astype(jnp.bfloat16).reshape(2, 4, rows, 256)
        return carry

    lax.fori_loop(0, channels // 256, grad_step, 0)
    order = z_peers + [z]
    over_y = [
        push(part.at[yn, zp], yin.at[d], to_y) for d, zp in enumerate(order)
    ]

    for copy in w_y:
        copy.wait_recv()
    weight = wgrp.reshape(8 * rows, channels)
    where = ((0, c, x, None), (1, c, xn, to_x), (2, cn, x, to_c), (3, cn, xn, to_cx))
    backs = []
    for slot, cc, xx, peer in where:
        value = lax.dot_general(
            weight[...], cotg[slot], (((1,), (1,)), ((), ())),
            preferred_element_type=jnp.float32,
        ).astype(jnp.bfloat16).reshape(2, 4, rows, frames)
        if peer is None:
            back_t[:, c, :, x] = value
        else:
            back_out[slot - 1] = value
            backs.append(push(back_out.at[slot - 1], back_t.at[:, c, :, x], peer))

    acts[...] = jnp.transpose(lhs.astype(jnp.float32)).astype(jnp.bfloat16)

    def out_step(i, carry):
        t = pl.ds(pl.multiple_of(i * 256, 256), 256)
        value = jnp.dot(acts[...], weight[:, t], preferred_element_type=jnp.float32)
        opart[:, :, t] = value.astype(jnp.bfloat16).reshape(4, frames, 256)
        return carry

    lax.fori_loop(0, channels // 256, out_step, 0)
    out_c = push(opart.at[2:4], oin, to_c)

    over_z = []

    def pass_on(d):
        over_y[d].wait_recv()
        added = part[y, order[d]].astype(jnp.float32) + yin[d].astype(jnp.float32)
        if d < 3:
            ysum[d] = added.astype(jnp.bfloat16)
            over_z.append(push(ysum.at[d], zin.at[d], (dp, order[d] * 2 + x)))
        else:
            wg_ref[...] = added

    pass_on(0)

    for copy in backs:
        copy.wait_recv()
    for g in range(4):
        t = slice(g * group, (g + 1) * group)
        piece = back_t[g // 2, g % 2].reshape(group, frames).astype(jnp.float32)
        grad = jnp.transpose(piece) * slope[:, t]
        slope[:, t] = grad
        one = jnp.sum(grad, axis=0, keepdims=True)
        two = jnp.sum(grad * normed[:, t], axis=0, keepdims=True)
        for j in range(group // LANE):
            cut = slice(j * LANE, (j + 1) * LANE)
            at = g * (group // LANE) + j
            stat[1, at : at + 1, :] = one[:, cut]
            stat[1, chunks + at : chunks + at + 1, :] = two[:, cut]
    second = sum_seq(1)

    out_c.wait_recv()
    osend[...] = (opart[1].astype(jnp.float32) + oin[1].astype(jnp.float32)).astype(jnp.bfloat16)
    out_x = push(osend, ox, to_x)
    osum[...] = opart[0].astype(jnp.float32) + oin[0].astype(jnp.float32)

    pass_on(1)
    second = sum_dp(1, second)
    pass_on(2)
    stat_res[1] = finish(1, second)

    def grad_conv_step(i, carry):
        t = tile(i)
        inverse = stat_res[0, pl.ds(chunks + i, 1), :]
        shift = stat_res[1, pl.ds(i, 1), :]
        scale = stat_res[1, pl.ds(chunks + i, 1), :]
        grad = valid * inverse * (slope[:, t] - shift - normed[:, t] * scale)
        gext[half : half + frames, t] = grad.astype(jnp.bfloat16)
        return carry

    lax.fori_loop(0, chunks, grad_conv_step, 0)
    halo = [
        push(gext.at[frames : frames + half], gext.at[0:half], seq_up),
        push(gext.at[half : 2 * half], gext.at[half + frames : frames + 2 * half], seq_down),
    ]
    pass_on(3)
    out_x.wait_recv()
    out_ref[...] = (osum[...] + ox[...].astype(jnp.float32)).astype(jnp.bfloat16)
    leave = [pltpu.make_async_copy(out_ref, out_hbm, local.at[0])]
    leave[0].start()
    for copy in halo:
        copy.wait_recv()

    def input_step(i, carry):
        t = tile(i)
        xf[:, t] = jnp.where(inside, gext[:, t].astype(jnp.float32), 0.0)
        weights = tap_ref[:, t]
        total = jnp.zeros((frames, LANE), jnp.float32)
        for k in range(taps):
            total = total + xf[2 * half - k : 2 * half - k + frames, t] * weights[k : k + 1]
        ig_ref[:, t] = (total * valid).astype(jnp.bfloat16)
        return carry

    for g in range(4):
        lax.fori_loop(g * chunks // 4, (g + 1) * chunks // 4, input_step, 0)
        t = pl.ds(g * group, group)
        leave.append(pltpu.make_async_copy(ig_ref.at[:, t], ig_hbm.at[:, t], local.at[1 + g]))
        leave[-1].start()
    total = wg_ref[...]
    for d, copy in enumerate(over_z):
        copy.wait_recv()
        total = total + zin[d].astype(jnp.float32)
    wg_ref[...] = total
    leave.append(pltpu.make_async_copy(wg_ref, wg_hbm, local.at[5]))
    leave[-1].start()
    for copy in leave:
        copy.wait()
    for copy in pending:
        copy.wait_send()


COPIES = 64


def hand_over(a_in, b_in, c_in, a_out, b_out, c_out):
    a_out[...] = a_in[...]
    b_out[...] = b_in[...]
    c_out[...] = c_in[...]


def on_device_fused(glu_out, conv_weight, bn_gain, bn_bias, w_out, cotangent, language, length):
    _, frames, channels = glu_out.shape
    rows = w_out.shape[0]
    half = conv_weight.shape[0] // 2
    bf16, f32 = jnp.bfloat16, jnp.float32
    stats = 2 * channels // LANE
    vmem = pl.BlockSpec(memory_space=pltpu.VMEM)
    hbm = pl.BlockSpec(memory_space=pltpu.HBM)
    smem = pl.BlockSpec(memory_space=pltpu.SMEM)
    results = (
        jax.ShapeDtypeStruct((frames, channels), bf16),
        jax.ShapeDtypeStruct((rows, channels), f32),
        jax.ShapeDtypeStruct((frames, channels), bf16),
    )
    made = pl.pallas_call(
        fused,
        out_shape=results,
        in_specs=[smem, smem] + [hbm] * 6,
        out_specs=(hbm, hbm, hbm),
        scratch_shapes=[
            pltpu.VMEM((frames, channels), bf16),
            pltpu.VMEM((rows, channels), f32),
            pltpu.VMEM((frames, channels), bf16),
            pltpu.VMEM(conv_weight.shape, f32),
            pltpu.VMEM(bn_gain.shape, f32),
            pltpu.VMEM(bn_bias.shape, f32),
            pltpu.VMEM((2, 4, rows, channels), bf16),
            pltpu.VMEM((4, frames, channels), bf16),
            pltpu.VMEM((frames, channels), bf16),
            pltpu.VMEM((2, 2, 4, 2, rows, frames), bf16),
            pltpu.VMEM((4, 2, 4, rows, frames), bf16),
            pltpu.VMEM((4 * frames, channels // 4), bf16),
            pltpu.VMEM((2, 2, 4, 2, rows, frames), bf16),
            pltpu.VMEM((3, 2, 4, rows, frames), bf16),
            pltpu.VMEM((4, frames, channels), bf16),
            pltpu.VMEM((2, frames, channels), bf16),
            pltpu.VMEM((frames, channels), f32),
            pltpu.VMEM((frames, channels), bf16),
            pltpu.VMEM((frames, channels), bf16),
            pltpu.VMEM((2, 4, rows, channels), bf16),
            pltpu.VMEM((3, rows, channels), bf16),
            pltpu.VMEM((4, rows, channels), bf16),
            pltpu.VMEM((3, rows, channels), bf16),
            pltpu.VMEM((frames + 2 * half, channels), bf16),
            pltpu.VMEM((frames + 2 * half, channels), f32),
            pltpu.VMEM((frames, channels), f32),
            pltpu.VMEM((frames, channels), f32),
            pltpu.VMEM((frames + 2 * half, channels), bf16),
            pltpu.VMEM((16, LANE), jnp.int32),
            pltpu.VMEM((3, 16, LANE), jnp.int32),
            pltpu.VMEM((2, stats, LANE), f32),
            pltpu.VMEM((2, 7, stats, LANE), f32),
            pltpu.VMEM((2, stats, LANE), f32),
            pltpu.VMEM((2, 3, stats, LANE), f32),
            pltpu.VMEM((2, stats, LANE), f32),
            pltpu.SemaphoreType.DMA((6,)),
            pltpu.SemaphoreType.DMA((COPIES,)),
            pltpu.SemaphoreType.DMA((COPIES,)),
        ],
        compiler_params=pltpu.CompilerParams(
            collective_id=0, has_side_effects=True, vmem_limit_bytes=62 * 1024 * 1024
        ),
    )(language, length, glu_out[0], conv_weight, bn_gain, bn_bias, w_out, cotangent[0])
    block_out, weight_grad, input_grad = pl.pallas_call(
        hand_over,
        out_shape=results,
        in_specs=[vmem] * 3,
        out_specs=(vmem, vmem, vmem),
        compiler_params=pltpu.CompilerParams(vmem_limit_bytes=62 * 1024 * 1024),
    )(*made)
    return block_out[None], weight_grad, input_grad[None]


def solution(mesh):
    placed = (
        P("dp", "seq", None),
        P(),
        P(),
        P(),
        P(("dp", "seq"), None),
        P("dp", "seq", None),
        P("dp"),
        P("dp"),
    )
    small = mesh.shape["dp"] == 4 and mesh.shape["seq"] == 8
    return jax.shard_map(
        on_device_fused if small else on_device,
        mesh=mesh,
        in_specs=placed,
        out_specs=(P("dp", "seq", None), P(("dp", "seq"), None), P("dp", "seq", None)),
        check_vma=False,
    )
```

```python
import jax
import jax.numpy as jnp
from jax import lax
from jax.experimental import pallas as pl
from jax.experimental.pallas import tpu as pltpu
from jax.sharding import PartitionSpec as P

LANGS = 16


epsilon = 1e-05


def with_halo(array, sides, width):
    for axis, dim in sides:
        size, length = (lax.axis_size(axis), array.shape[dim])
        up = [(i, (i + 1) % size) for i in range(size - 1)]
        down = [(j, i) for i, j in up]
        last = lax.slice_in_dim(array, length - width, length, axis=dim)
        first = lax.slice_in_dim(array, 0, width, axis=dim)
        before = lax.ppermute(last, axis, up)
        after = lax.ppermute(first, axis, down)
        array = jnp.concatenate([before, array, after], axis=dim)
    return array


def depthwise(padded, taps, frames):
    running = jnp.zeros((padded.shape[0], frames, padded.shape[2]), jnp.float32)
    for offset in range(taps.shape[0]):
        running = running + padded[:, offset : offset + frames].astype(jnp.float32) * taps[offset]
    return running


def with_rim(values, half_width):
    return with_halo(values, (("seq", 1),), half_width)


def per_language(one_hot, values_table):
    return jnp.dot(one_hot.T, values_table, precision=lax.Precision.HIGHEST)


def per_utterance(one_hot, values_table):
    return jnp.dot(one_hot, values_table, precision=lax.Precision.HIGHEST)[:, None, :]


def on_device(glu_out, conv_weight, bn_gain, bn_bias, w_out, cotangent, language, length):
    utterances, frames, channels = glu_out.shape
    kernel = conv_weight.shape[0]
    half_width = kernel // 2
    position = lax.axis_index("seq") * frames + lax.iota(jnp.int32, frames)
    valid = (position[None, :] < length[:, None]).astype(jnp.float32)[:, :, None]
    one_hot = (language[:, None] == lax.iota(jnp.int32, LANGS)[None, :]).astype(jnp.float32)
    masked = glu_out * valid.astype(jnp.bfloat16)
    extended = with_rim(masked, half_width)
    convolved = depthwise(extended[:, : frames + kernel - 1], conv_weight, frames)
    counts = per_language(one_hot, jnp.sum(valid, axis=(1, 2)))
    local_sum = per_language(one_hot, jnp.sum(convolved * valid, axis=1))
    local_square = per_language(one_hot, jnp.sum(convolved * convolved * valid, axis=1))
    total_sum, total_square, total_count = lax.psum(
        (local_sum, local_square, counts), ("dp", "seq")
    )
    denominator = jnp.maximum(total_count, 1.0)[:, None]
    average = total_sum / denominator
    variance = total_square / denominator - average * average
    average_utt = per_utterance(one_hot, average)
    inverse_utt = per_utterance(one_hot, lax.rsqrt(variance + epsilon))
    gain_utt = per_utterance(one_hot, bn_gain)
    bias_utt = per_utterance(one_hot, bn_bias)
    normed = (convolved - average_utt) * inverse_utt
    pre_act = normed * gain_utt + bias_utt
    sigmoid_act = jax.nn.sigmoid(pre_act)
    active = (pre_act * sigmoid_act * valid).astype(jnp.bfloat16)
    full_weight = lax.all_gather(w_out, ("dp", "seq"), axis=0, tiled=True)
    flat_active = active.reshape(utterances * frames, channels)
    flat_grad = cotangent.reshape(utterances * frames, channels)
    output = jnp.dot(flat_active, full_weight, preferred_element_type=jnp.float32)
    output = output.astype(jnp.bfloat16).reshape(utterances, frames, channels)
    back_proj = lax.dot_general(
        flat_grad, full_weight, (((1,), (1,)), ((), ())), preferred_element_type=jnp.float32
    )
    back_proj = back_proj.reshape(utterances, frames, channels)
    grad_pre = back_proj * valid * sigmoid_act * (1.0 + pre_act * (1.0 - sigmoid_act))
    grad_normed = grad_pre * gain_utt
    first_sum, second_sum = lax.psum(
        (
            per_language(one_hot, jnp.sum(grad_normed, axis=1)),
            per_language(one_hot, jnp.sum(grad_normed * normed, axis=1)),
        ),
        ("dp", "seq"),
    )
    shift_term = per_utterance(one_hot, first_sum / denominator)
    scale_term = per_utterance(one_hot, second_sum / denominator)
    grad_conv = (valid * inverse_utt * (grad_normed - shift_term - normed * scale_term)).astype(
        jnp.bfloat16
    )
    rim_grad = with_rim(grad_conv, half_width)
    input_grad = (depthwise(rim_grad[:, 1:], conv_weight[::-1], frames) * valid).astype(
        jnp.bfloat16
    )
    weight_grad = lax.psum_scatter(
        lax.dot_general(
            flat_active, flat_grad, (((0,), (0,)), ((), ())), preferred_element_type=jnp.float32
        ),
        ("dp", "seq"),
        scatter_dimension=0,
        tiled=True,
    )
    return (output, weight_grad, input_grad)


MESH = pl.DeviceIdType.MESH
LANE = 128


def tile(c):
    return pl.ds(pl.multiple_of(c * LANE, LANE), LANE)


def fused(
    lang_ref, len_ref, x_hbm, tap_hbm, gain_hbm, bias_hbm, w_hbm, cot_hbm,
    out_ref, wg_ref, ig_ref,
    tap_ref, gain_ref, bias_ref, wgrp, cotg, act, act_t, ag, acts, back_t, back_out,
    opart, oin, osum, osend, ox, part, ysum, yin, zin,
    ext, xf, normed, slope, gext,
    info, info_in, stat, stat_in, stat_mid, stat_dp, stat_res,
    local, send, recv,
):
    frames, channels = x_hbm.shape
    taps = tap_ref.shape[0]
    half = taps // 2
    chunks = channels // LANE
    dp, seq = lax.axis_index("dp"), lax.axis_index("seq")
    y, c, z, x = dp // 2, dp % 2, seq // 2, seq % 2
    seq_x, dp_c, dp_y = seq + 1 - 2 * x, dp + 1 - 2 * c, dp + 2 - 4 * y
    to_x, to_c, to_y, to_cx = (dp, seq_x), (dp_c, seq), (dp_y, seq), (dp_c, seq_x)
    xn, cn, yn = 1 - x, 1 - c, 1 - y
    seq_peers = [(dp, (seq + d) % 8) for d in range(1, 8)]
    dp_peers = [((dp + d) % 4, seq) for d in range(1, 4)]
    z_peers = [(z + d) % 4 for d in range(1, 4)]
    lang, length = lang_ref[0], len_ref[0]

    barrier = pltpu.get_barrier_semaphore()
    greet = seq_peers + dp_peers + [to_cx]
    for peer in greet:
        pl.semaphore_signal(barrier, inc=1, device_id=peer, device_id_type=MESH)

    own = [
        pltpu.make_async_copy(src, dst, local.at[i])
        for i, (src, dst) in enumerate((
            (x_hbm, ext.at[half : half + frames]),
            (w_hbm, wgrp.at[y, z]),
            (cot_hbm, cotg.at[0]),
            (tap_hbm, tap_ref),
            (gain_hbm, gain_ref),
            (bias_hbm, bias_ref),
        ))
    ]
    for copy in own:
        copy.start()
    info[0:8, :] = jnp.full((8, LANE), lang, jnp.int32)
    info[8:16, :] = jnp.full((8, LANE), length, jnp.int32)
    for copy in own:
        copy.wait()
    pl.semaphore_wait(barrier, len(greet))

    pending = []
    count = [0]

    def push(src, dst, peer):
        i = count[0]
        count[0] += 1
        copy = pltpu.make_async_remote_copy(
            src_ref=src, dst_ref=dst, send_sem=send.at[i], recv_sem=recv.at[i],
            device_id=peer, device_id_type=MESH,
        )
        copy.start()
        pending.append(copy)
        return copy

    seq_up, seq_down = (dp, (seq + 1) % 8), (dp, (seq + 7) % 8)
    halo = [
        push(ext.at[frames : frames + half], ext.at[0:half], seq_up),
        push(ext.at[half : 2 * half], ext.at[half + frames : frames + 2 * half], seq_down),
    ]
    w_z = [push(wgrp.at[y, z], wgrp.at[y, z], (dp, zp * 2 + x)) for zp in z_peers]
    w_y = [push(wgrp.at[y, z], wgrp.at[y, z], to_y)]
    cot_x = push(cotg.at[0], cotg.at[1], to_x)
    cot_c = push(cotg.at[0], cotg.at[2], to_c)
    told = [push(info, info_in.at[d], peer) for d, peer in enumerate(dp_peers)]

    row = lax.broadcasted_iota(jnp.int32, (frames + 2 * half, LANE), 0) + (seq * frames - half)
    inside = (row >= 0) & (row < length)
    valid = inside[half : half + frames].astype(jnp.float32)

    for copy in halo:
        copy.wait_recv()

    def conv_step(i, carry):
        t = tile(i)
        xf[:, t] = jnp.where(inside, ext[:, t].astype(jnp.float32), 0.0)
        weights = tap_ref[:, t]
        total = jnp.zeros((frames, LANE), jnp.float32)
        for k in range(taps):
            total = total + xf[k : k + frames, t] * weights[k : k + 1]
        normed[:, t] = total
        kept = total * valid
        stat[0, pl.ds(i, 1), :] = jnp.sum(kept, axis=0, keepdims=True)
        stat[0, pl.ds(chunks + i, 1), :] = jnp.sum(kept * total, axis=0, keepdims=True)
        return carry

    lax.fori_loop(0, chunks, conv_step, 0)

    def sum_seq(n):
        return [push(stat.at[n], stat_in.at[n, d], peer) for d, peer in enumerate(seq_peers)]

    def sum_dp(n, copies):
        for copy in copies:
            copy.wait_recv()
        total = stat[n]
        for d in range(7):
            total = total + stat_in[n, d]
        stat_mid[n] = total
        return [push(stat_mid.at[n], stat_dp.at[n, d], peer) for d, peer in enumerate(dp_peers)]

    def finish(n, copies):
        for copy in copies:
            copy.wait_recv()
        total = stat_mid[n]
        frames_of = jnp.full((1, LANE), length, jnp.int32).astype(jnp.float32)
        for d in range(3):
            same = (info_in[d, 0:1, :] == lang).astype(jnp.float32)
            total = total + stat_dp[n, d] * same
            frames_of = frames_of + info_in[d, 8:9, :].astype(jnp.float32) * same
        return total / jnp.maximum(frames_of, 1.0)

    first = sum_seq(0)

    first = sum_dp(0, first)
    for d in range(3):
        w_z[d].wait_recv()
        block = wgrp.at[y, (z + 3 - d) % 4]
        w_y.append(push(block, block, to_y))
    cot_x.wait_recv()
    cot_cx = push(cotg.at[1], cotg.at[3], to_c)
    for copy in told:
        copy.wait_recv()
    mean = finish(0, first)
    average = mean[0:chunks]
    variance = mean[chunks : 2 * chunks] - average * average
    stat_res[0, 0:chunks, :] = average
    stat_res[0, chunks : 2 * chunks, :] = lax.rsqrt(variance + epsilon)

    mine = lax.broadcasted_iota(jnp.int32, (LANGS, LANE), 0) == lang

    def act_step(i, carry):
        t = tile(i)
        average = stat_res[0, pl.ds(i, 1), :]
        inverse = stat_res[0, pl.ds(chunks + i, 1), :]
        gain = jnp.sum(jnp.where(mine, gain_ref[:, t], 0.0), axis=0, keepdims=True)
        bias = jnp.sum(jnp.where(mine, bias_ref[:, t], 0.0), axis=0, keepdims=True)
        norm = (normed[:, t] - average) * inverse
        pre = norm * gain + bias
        s = jax.nn.sigmoid(pre)
        normed[:, t] = norm
        slope[:, t] = valid * s * (1.0 + pre * (1.0 - s)) * gain
        act[:, t] = (pre * s * valid).astype(jnp.bfloat16)
        return carry

    lax.fori_loop(0, chunks, act_step, 0)

    group = channels // 4
    rows = wg_ref.shape[0]
    for g in range(4):
        turned = jnp.transpose(act[:, g * group : (g + 1) * group].astype(jnp.float32))
        act_t[g // 2, g % 2] = turned.astype(jnp.bfloat16).reshape(4, 2, rows, frames)

    factors = [
        push(act_t.at[:, cc, :, xx], ag.at[slot], peer)
        for slot, cc, xx, peer in ((1, c, xn, to_x), (2, cn, x, to_c), (3, cn, xn, to_cx))
    ]
    ag[0] = act_t[:, c, :, x]

    cot_c.wait_recv()
    cot_cx.wait_recv()
    for copy in factors:
        copy.wait_recv()
    lhs = jnp.concatenate([ag[s].reshape(8 * rows, frames) for s in range(4)], axis=1)
    rhs = cotg.reshape(4 * frames, channels)

    def grad_step(i, carry):
        t = pl.ds(pl.multiple_of(i * 256, 256), 256)
        value = jnp.dot(lhs, rhs[:, t], preferred_element_type=jnp.float32)
        part[:, :, :, t] = value.astype(jnp.bfloat16).reshape(2, 4, rows, 256)
        return carry

    lax.fori_loop(0, channels // 256, grad_step, 0)
    order = z_peers + [z]
    over_y = [
        push(part.at[yn, zp], yin.at[d], to_y) for d, zp in enumerate(order)
    ]

    for copy in w_y:
        copy.wait_recv()
    weight = wgrp.reshape(8 * rows, channels)
    where = ((0, c, x, None), (1, c, xn, to_x), (2, cn, x, to_c), (3, cn, xn, to_cx))
    backs = []
    for slot, cc, xx, peer in where:
        value = lax.dot_general(
            weight[...], cotg[slot], (((1,), (1,)), ((), ())),
            preferred_element_type=jnp.float32,
        ).astype(jnp.bfloat16).reshape(2, 4, rows, frames)
        if peer is None:
            back_t[:, c, :, x] = value
        else:
            back_out[slot - 1] = value
            backs.append(push(back_out.at[slot - 1], back_t.at[:, c, :, x], peer))

    acts[...] = jnp.transpose(lhs.astype(jnp.float32)).astype(jnp.bfloat16)

    def out_step(i, carry):
        t = pl.ds(pl.multiple_of(i * 256, 256), 256)
        value = jnp.dot(acts[...], weight[:, t], preferred_element_type=jnp.float32)
        opart[:, :, t] = value.astype(jnp.bfloat16).reshape(4, frames, 256)
        return carry

    lax.fori_loop(0, channels // 256, out_step, 0)
    out_c = push(opart.at[2:4], oin, to_c)

    over_z = []

    def pass_on(d):
        over_y[d].wait_recv()
        added = part[y, order[d]].astype(jnp.float32) + yin[d].astype(jnp.float32)
        if d < 3:
            ysum[d] = added.astype(jnp.bfloat16)
            over_z.append(push(ysum.at[d], zin.at[d], (dp, order[d] * 2 + x)))
        else:
            wg_ref[...] = added

    pass_on(0)

    for copy in backs:
        copy.wait_recv()
    for g in range(4):
        t = slice(g * group, (g + 1) * group)
        piece = back_t[g // 2, g % 2].reshape(group, frames).astype(jnp.float32)
        grad = jnp.transpose(piece) * slope[:, t]
        slope[:, t] = grad
        one = jnp.sum(grad, axis=0, keepdims=True)
        two = jnp.sum(grad * normed[:, t], axis=0, keepdims=True)
        for j in range(group // LANE):
            cut = slice(j * LANE, (j + 1) * LANE)
            at = g * (group // LANE) + j
            stat[1, at : at + 1, :] = one[:, cut]
            stat[1, chunks + at : chunks + at + 1, :] = two[:, cut]
    second = sum_seq(1)

    out_c.wait_recv()
    osend[...] = (opart[1].astype(jnp.float32) + oin[1].astype(jnp.float32)).astype(jnp.bfloat16)
    out_x = push(osend, ox, to_x)
    osum[...] = opart[0].astype(jnp.float32) + oin[0].astype(jnp.float32)

    pass_on(1)
    second = sum_dp(1, second)
    pass_on(2)
    stat_res[1] = finish(1, second)

    def grad_conv_step(i, carry):
        t = tile(i)
        inverse = stat_res[0, pl.ds(chunks + i, 1), :]
        shift = stat_res[1, pl.ds(i, 1), :]
        scale = stat_res[1, pl.ds(chunks + i, 1), :]
        grad = valid * inverse * (slope[:, t] - shift - normed[:, t] * scale)
        gext[half : half + frames, t] = grad.astype(jnp.bfloat16)
        return carry

    lax.fori_loop(0, chunks, grad_conv_step, 0)
    halo = [
        push(gext.at[frames : frames + half], gext.at[0:half], seq_up),
        push(gext.at[half : 2 * half], gext.at[half + frames : frames + 2 * half], seq_down),
    ]
    pass_on(3)
    for copy in halo:
        copy.wait_recv()

    def input_step(i, carry):
        t = tile(i)
        xf[:, t] = jnp.where(inside, gext[:, t].astype(jnp.float32), 0.0)
        weights = tap_ref[:, t]
        total = jnp.zeros((frames, LANE), jnp.float32)
        for k in range(taps):
            total = total + xf[2 * half - k : 2 * half - k + frames, t] * weights[k : k + 1]
        ig_ref[:, t] = (total * valid).astype(jnp.bfloat16)
        return carry

    lax.fori_loop(0, chunks, input_step, 0)
    out_x.wait_recv()
    out_ref[...] = (osum[...] + ox[...].astype(jnp.float32)).astype(jnp.bfloat16)
    total = wg_ref[...]
    for d, copy in enumerate(over_z):
        copy.wait_recv()
        total = total + zin[d].astype(jnp.float32)
    wg_ref[...] = total
    for copy in pending:
        copy.wait_send()


COPIES = 64


def on_device_fused(glu_out, conv_weight, bn_gain, bn_bias, w_out, cotangent, language, length):
    _, frames, channels = glu_out.shape
    rows = w_out.shape[0]
    half = conv_weight.shape[0] // 2
    bf16, f32 = jnp.bfloat16, jnp.float32
    stats = 2 * channels // LANE
    vmem = pl.BlockSpec(memory_space=pltpu.VMEM)
    smem = pl.BlockSpec(memory_space=pltpu.SMEM)
    block_out, weight_grad, input_grad = pl.pallas_call(
        fused,
        out_shape=(
            jax.ShapeDtypeStruct((frames, channels), bf16),
            jax.ShapeDtypeStruct((rows, channels), f32),
            jax.ShapeDtypeStruct((frames, channels), bf16),
        ),
        in_specs=[smem, smem] + [pl.BlockSpec(memory_space=pltpu.HBM)] * 6,
        out_specs=(vmem, vmem, vmem),
        scratch_shapes=[
            pltpu.VMEM(conv_weight.shape, f32),
            pltpu.VMEM(bn_gain.shape, f32),
            pltpu.VMEM(bn_bias.shape, f32),
            pltpu.VMEM((2, 4, rows, channels), bf16),
            pltpu.VMEM((4, frames, channels), bf16),
            pltpu.VMEM((frames, channels), bf16),
            pltpu.VMEM((2, 2, 4, 2, rows, frames), bf16),
            pltpu.VMEM((4, 2, 4, rows, frames), bf16),
            pltpu.VMEM((4 * frames, channels // 4), bf16),
            pltpu.VMEM((2, 2, 4, 2, rows, frames), bf16),
            pltpu.VMEM((3, 2, 4, rows, frames), bf16),
            pltpu.VMEM((4, frames, channels), bf16),
            pltpu.VMEM((2, frames, channels), bf16),
            pltpu.VMEM((frames, channels), f32),
            pltpu.VMEM((frames, channels), bf16),
            pltpu.VMEM((frames, channels), bf16),
            pltpu.VMEM((2, 4, rows, channels), bf16),
            pltpu.VMEM((3, rows, channels), bf16),
            pltpu.VMEM((4, rows, channels), bf16),
            pltpu.VMEM((3, rows, channels), bf16),
            pltpu.VMEM((frames + 2 * half, channels), bf16),
            pltpu.VMEM((frames + 2 * half, channels), f32),
            pltpu.VMEM((frames, channels), f32),
            pltpu.VMEM((frames, channels), f32),
            pltpu.VMEM((frames + 2 * half, channels), bf16),
            pltpu.VMEM((16, LANE), jnp.int32),
            pltpu.VMEM((3, 16, LANE), jnp.int32),
            pltpu.VMEM((2, stats, LANE), f32),
            pltpu.VMEM((2, 7, stats, LANE), f32),
            pltpu.VMEM((2, stats, LANE), f32),
            pltpu.VMEM((2, 3, stats, LANE), f32),
            pltpu.VMEM((2, stats, LANE), f32),
            pltpu.SemaphoreType.DMA((6,)),
            pltpu.SemaphoreType.DMA((COPIES,)),
            pltpu.SemaphoreType.DMA((COPIES,)),
        ],
        compiler_params=pltpu.CompilerParams(
            collective_id=0, has_side_effects=True, vmem_limit_bytes=62 * 1024 * 1024
        ),
    )(language, length, glu_out[0], conv_weight, bn_gain, bn_bias, w_out, cotangent[0])
    return block_out[None], weight_grad, input_grad[None]


def solution(mesh):
    placed = (
        P("dp", "seq", None),
        P(),
        P(),
        P(),
        P(("dp", "seq"), None),
        P("dp", "seq", None),
        P("dp"),
        P("dp"),
    )
    small = mesh.shape["dp"] == 4 and mesh.shape["seq"] == 8
    return jax.shard_map(
        on_device_fused if small else on_device,
        mesh=mesh,
        in_specs=placed,
        out_specs=(P("dp", "seq", None), P(("dp", "seq"), None), P("dp", "seq", None)),
        check_vma=False,
    )
```
